128 devices in a mesh: pair: 8 (over z_hi, x), blk: 16 (over y, z_lo, core).
Axes of the slice: x: 4, y: 4, z: 4 (z_hi: 2, z_lo: 2; z = z_hi * 2 + z_lo), core: 2. Of those that a mesh axis runs over, the one named last changes fastest.
Arguments:
- queries: bfloat16 [8, 2048, 4096], P('pair', 'blk')
- prompt_keys: bfloat16 [8, 4096, 512], P('pair', 'blk')
- prompt_values: bfloat16 [8, 4096, 512], P('pair', 'blk'), may hold values from -6 to 6
- resp_keys: bfloat16 [8, 2048, 512], P('pair', 'blk'), may hold values from -6 to 6
- resp_values: bfloat16 [8, 2048, 512], P('pair', 'blk'), may hold values from -6 to 6
- slot_row: int32 [8, 2048], P('pair', 'blk'), may hold values from -1 to 1023, as said below
- lengths: int32 [8, 2], P('pair'), may hold values from 1 to 768, 1024 in all within a row
- probe: float32 [4096], replicated, may hold values from -6 to 6
Outputs:
- attended: bfloat16 [8, 2048, 4096], P('pair', 'blk')
- loss: float32 [], replicated
The draws below stay inside these ranges and needn't reach their ends.
Inputs may be any that keep to these rules, and one draw needn't show every extreme that they name: `slot_row`: in each pair every response row 0 to 1023 stands in exactly one slot; the other slots hold -1. On each device the live slots come first. The live slots of a device and of the device half the blk axis away number 2 * 64 together, and some device of each pair has all 128 slots live.
All inputs are finite; a program needn't handle non-finite values.
Results may differ from the reference program's by a relative error of at most 0.024.
Values may be sent and summed in bfloat16 or wider, within the bound.
A program may use at most 128 MiB of HBM per device.

```python
import math
import jax
import jax.numpy as jnp
import numpy as np
from jax import lax

QH = 32
KVH = 4
HD = 128
BAL = 64
SLOT_DEV = 128
PAIRS = 8
PROMPT = 4096
SLOTS = 2048
RESP = 1024
LONGEST = 768
N_BLK = 16


def shared_keys(key):
    return jax.random.normal(key, (PAIRS, PROMPT, KVH * HD), jnp.float32)


def draw_prompt_keys(key, part):
    base = shared_keys(key)
    return base.astype(jnp.bfloat16)


def draw_queries(key, part):
    key = jax.random.fold_in(key, 11)
    base = jax.random.normal(key, (PAIRS, SLOTS, QH * HD), jnp.float32)
    return base.astype(jnp.bfloat16)


def draw_slot_row(key, part):
    key = jax.random.fold_in(key, 23)
    key_shift, key_pick, key_order = jax.random.split(key, 3)
    half = N_BLK // 2
    shift = jax.random.randint(key_shift, (PAIRS, half), -BAL, BAL + 1)
    pick = jax.random.randint(key_pick, (PAIRS,), 0, half)
    shift = jnp.where(jnp.arange(half)[None, :] == pick[:, None], BAL, shift)
    loads = jnp.concatenate([BAL + shift, BAL - shift], axis=1)
    starts = jnp.cumsum(loads, axis=1) - loads
    order_keys = jax.random.split(key_order, PAIRS)
    orders = jax.vmap(lambda single: jax.random.permutation(single, RESP))(order_keys)
    place = jnp.arange(SLOT_DEV)
    live = place[None, None, :] < loads[:, :, None]
    index = jnp.clip(starts[:, :, None] + place[None, None, :], 0, RESP - 1).reshape(PAIRS, -1)
    rows = jnp.take_along_axis(orders, index, axis=1).reshape(PAIRS, N_BLK, SLOT_DEV)
    rows = jnp.where(live, rows, -1)
    return rows.reshape(PAIRS, SLOTS).astype(jnp.int32)


def steps_of(key, shape, shards, low, high):
    gain = 1.0
    for position, shards_of in shards:
        draws = jax.random.uniform(jax.random.fold_in(jax.random.fold_in(key, 6), position), (shards_of,), jnp.float32, low / len(shards), high / len(shards))
        gain = gain * jnp.repeat(jnp.exp(draws), shape[position] // shards_of).reshape((-1,) + (1,) * (len(shape) - 1 - position))
    return gain


def length_profile(count, total, limit, skew):
    weights = [(1 << 20) // math.isqrt(grade ** skew) + 1 for grade in range(2, count + 1)]
    rest, given = total - limit - (count - 1), [1] * (count - 1)
    while rest > 0:
        movable = [i for i in range(count - 1) if given[i] < limit]
        pool, remaining = sum([weights[i] for i in movable]), rest
        for i in movable:
            addition = min(limit - given[i], max(1, remaining * weights[i] // pool), rest)
            given[i] = given[i] + addition
            rest = rest - addition
    return np.array([limit] + given)


def uneven(stream_key, count, total, bound, lean):
    if count == 2:
        one = jax.random.randint(stream_key, (), max(1, total - bound), min(bound, total - 1) + 1)
        return jnp.stack([one, total - one])
    tallies = jnp.asarray(length_profile(count, total, bound, lean), jnp.int32)
    couples = (count - 1) // 2
    donor, sink = tallies[1:1 + 2 * couples:2], tallies[2:2 + 2 * couples:2]
    slack = jnp.minimum(donor - 1, bound - sink)
    shifted = jax.random.randint(jax.random.fold_in(stream_key, 1), (couples,), 0, 1 << 20) % (slack + 1)
    tallies = tallies.at[1:1 + 2 * couples:2].set(donor - shifted).at[2:2 + 2 * couples:2].set(sink + shifted)
    return tallies[jax.random.permutation(jax.random.fold_in(stream_key, 2), count)]


def gaussian(own_key, extent, scale, most, pieces=(), dtype=jnp.bfloat16):
    gain = steps_of(own_key, extent, pieces, -0.22, 0.18) if pieces else 1.0
    drawn = jax.random.normal(own_key, extent, jnp.float32) * scale * gain
    return jnp.minimum(jnp.maximum(drawn, -most), most).astype(dtype)


def setup_inputs(seed: int = 0) -> dict:
    key_of = jax.random.split(jax.random.key(seed), 9)
    queries = draw_queries(jax.random.fold_in(key_of[8], 71), 0)
    prompt_keys = draw_prompt_keys(jax.random.fold_in(key_of[8], 71), 0)
    prompt_values = gaussian(key_of[2], (PAIRS, PROMPT, KVH * HD), 1.0, 6.0, ((0, 8), (1, 16)))
    resp_keys = gaussian(key_of[3], (PAIRS, SLOTS, KVH * HD), 1.0, 6.0, ((0, 8), (1, 16)))
    resp_values = gaussian(key_of[4], (PAIRS, SLOTS, KVH * HD), 1.0, 6.0, ((0, 8), (1, 16)))
    slot_row = draw_slot_row(jax.random.fold_in(key_of[8], 71), 0)
    lengths = jax.vmap(lambda own: uneven(own, 2, RESP, LONGEST, 0))(jax.random.split(key_of[6], PAIRS)).reshape((PAIRS, 2)).astype(jnp.int32)
    probe = gaussian(key_of[7], (QH * HD,), 1.0, 6.0, (), jnp.float32)
    return dict(queries=queries, prompt_keys=prompt_keys, prompt_values=prompt_values, resp_keys=resp_keys, resp_values=resp_values, slot_row=slot_row, lengths=lengths, probe=probe)


def attend_pair(queries, prompt_keys, prompt_values, resp_keys, resp_values, slot_row, chosen_len):
    groups = QH // KVH
    keys = jnp.concatenate([prompt_keys, resp_keys], 0).astype(jnp.float32).reshape(-1, KVH, HD)
    values = jnp.concatenate([prompt_values, resp_values], 0).astype(jnp.float32).reshape(-1, KVH, HD)
    key_ids = jnp.concatenate([jnp.full((PROMPT,), -2, jnp.int32), slot_row])
    blocks = queries.reshape(SLOTS // SLOT_DEV, SLOT_DEV, QH * HD)
    row_blocks = slot_row.reshape(SLOTS // SLOT_DEV, SLOT_DEV)

    def one(args):
        query_block, query_ids = args
        rows = query_block.shape[0]
        q4 = query_block.astype(jnp.float32).reshape(rows, KVH, groups, HD)
        score = jnp.einsum('bkgd,nkd->bkgn', q4, keys) / jnp.sqrt(jnp.float32(HD))
        same = (key_ids[None, :] >= chosen_len) == (query_ids[:, None] >= chosen_len)
        earlier = (key_ids[None, :] >= 0) & (key_ids[None, :] <= query_ids[:, None]) & same
        visible = (key_ids[None, :] == -2) | earlier
        vis4 = visible[:, None, None, :]
        score = jnp.where(vis4, score, jnp.float32(-1e+30))
        top = lax.optimization_barrier(jnp.max(score, axis=-1, keepdims=True))
        raw = jnp.where(vis4, jnp.exp(score - top), jnp.float32(0.0))
        total = lax.optimization_barrier(jnp.sum(raw, axis=-1))
        weight = raw.astype(jnp.bfloat16).astype(jnp.float32)
        acc = jnp.einsum('bkgn,nkd->bkgd', weight, values)
        out = (acc / total[..., None]).reshape(rows, QH * HD)
        out = jnp.where((query_ids >= 0)[:, None], out, jnp.float32(0.0))
        return out.astype(jnp.bfloat16)
    return lax.map(one, (blocks, row_blocks)).reshape(SLOTS, QH * HD)

def reference(queries, prompt_keys, prompt_values, resp_keys, resp_values, slot_row, lengths, probe):
    outputs = []
    loss = jnp.float32(0.0)
    for pair_index in range(PAIRS):
        chosen_len = lengths[pair_index, 0]
        rejected_len = lengths[pair_index, 1]
        ids = slot_row[pair_index]
        attended = attend_pair(queries[pair_index], prompt_keys[pair_index], prompt_values[pair_index], resp_keys[pair_index], resp_values[pair_index], ids, chosen_len)
        outputs.append(attended)
        row_score = jnp.dot(attended.astype(jnp.float32), probe, precision=lax.Precision.HIGHEST)
        chosen = (ids >= 0) & (ids < chosen_len)
        rejected = ids >= chosen_len
        s_chosen = jnp.sum(jnp.where(chosen, row_score, jnp.float32(0.0))) / chosen_len.astype(jnp.float32)
        s_rejected = jnp.sum(jnp.where(rejected, row_score, jnp.float32(0.0))) / rejected_len.astype(jnp.float32)
        loss = loss + jax.nn.softplus(-4.0 * (s_chosen - s_rejected))
    return (jnp.stack(outputs), loss)
```

```python
import functools

import jax
import jax.numpy as jnp
from jax import lax
from jax.experimental import pallas as pl
from jax.experimental.pallas import tpu as pltpu
from jax.sharding import PartitionSpec as P

QH = 32
KVH = 4
HD = 128
GROUP = QH // KVH
SLOT = 128
PKEYS = 256
NY = 4
NBLK = 16
WIDE = GROUP * HD
SCALE = 1.4426950408889634 / HD**0.5
MESH = pl.DeviceIdType.MESH
BF = jnp.bfloat16
F32 = jnp.float32
LOW = -1e30
HIGH = 3e38


def dot_t(a, b):
    return lax.dot_general(a, b, (((1,), (1,)), ((), ())), preferred_element_type=F32)


def dot(a, b):
    return jnp.dot(a, b, preferred_element_type=F32)


def kernel(
    n_pair,
    q_hbm, kp_hbm, vp_hbm, kr_hbm, vr_hbm, slot_ref, len_ref, probe_ref,
    att_ref, loss_ref,
    kv, idb, qin, qs, krm, vrm, bias, qid, top, acc, score, osend, oin, part, term,
    local_sem, kv_send, kv_recv, z_send, z_recv, c_send, c_recv, zc_send, zc_recv,
    id_send, id_recv, q_send, q_recv, o_send, o_recv, p_send, p_recv, t_send, t_recv,
):
    pair = lax.axis_index("pair")
    blk = lax.axis_index("blk")
    y, z, c = blk // 4, (blk // 2) % 2, blk % 2

    def device(dy, dz, dc):
        return (pair, ((y + dy) % NY) * 4 + ((z + dz) % 2) * 2 + (c + dc) % 2)

    others = [(dy, dz, dc) for dz in range(2) for dc in range(2) for dy in range(NY)][1:]

    def remote(src, dst, send, recv, target):
        return pltpu.make_async_remote_copy(
            src_ref=src, dst_ref=dst, send_sem=send, recv_sem=recv,
            device_id=target, device_id_type=MESH,
        )

    def columns(head, width):
        return pl.ds(pl.multiple_of(head * width, width), width)

    def kv_parts(head, slot):
        cols = columns(head, HD)
        return (
            (kp_hbm.at[:, cols], kv.at[slot, pl.ds(0, PKEYS)]),
            (vp_hbm.at[:, cols], kv.at[slot, pl.ds(PKEYS, PKEYS)]),
            (kr_hbm.at[:, cols], kv.at[slot, pl.ds(2 * PKEYS, SLOT)]),
            (vr_hbm.at[:, cols], kv.at[slot, pl.ds(2 * PKEYS + SLOT, SLOT)]),
        )

    own = [pltpu.make_async_copy(s, d, local_sem.at[i]) for i, (s, d) in enumerate(kv_parts(y, y))]
    own_q = pltpu.make_async_copy(q_hbm.at[:, columns(y, WIDE)], qin.at[y], local_sem.at[4])
    for copy in own:
        copy.start()
    own_q.start()
    idb[y] = jnp.broadcast_to(slot_ref[...], (8, SLOT))

    barrier = pltpu.get_barrier_semaphore()
    for dy, dz, dc in others:
        pl.semaphore_signal(barrier, inc=1, device_id=device(dy, dz, dc), device_id_type=MESH)
    for d in range(1, n_pair):
        pl.semaphore_signal(
            barrier, inc=1, device_id=((pair + d) % n_pair, blk), device_id_type=MESH
        )
    pl.semaphore_wait(barrier, NBLK - 1 + n_pair - 1)

    kv_copies = {}
    for dy in (1, 3, 2):
        to = device(dy, 0, 0)
        for s, d in kv_parts((y + dy) % NY, y):
            remote(s, d, kv_send.at[dy], kv_recv.at[dy], to).start()
        kv_copies[dy] = remote(kv.at[y], kv.at[y], kv_send.at[dy], kv_recv.at[dy], to)
    id_copies = []
    for i, (dy, dz, dc) in enumerate(others):
        copy = remote(
            idb.at[y], idb.at[dz * 8 + dc * 4 + y], id_send.at[i], id_recv.at[i], device(dy, dz, dc)
        )
        copy.start()
        id_copies.append(copy)
    q_copies = {}
    for dy in (2, 1, 3):
        q_copies[dy] = remote(
            q_hbm.at[:, columns((y + dy) % NY, WIDE)], qin.at[y],
            q_send.at[dy], q_recv.at[dy], device(dy, 0, 0),
        )

    z_copies, c_copies, zc_copies = {}, {}, {}

    def forward(dy):
        at = (y - dy + NY) % NY
        z_copies[dy] = remote(
            kv.at[at], kv.at[8 + at], z_send.at[dy], z_recv.at[dy], device(0, 1, 0)
        )
        c_copies[dy] = remote(
            kv.at[at], kv.at[4 + at], c_send.at[dy], c_recv.at[dy], device(0, 0, 1)
        )
        z_copies[dy].start()
        c_copies[dy].start()

    for copy in own:
        copy.wait()
    forward(0)

    for copy in id_copies:
        copy.wait_recv()
    rows = lax.broadcasted_iota(jnp.int32, (SLOT, SLOT), 0)
    cols = lax.broadcasted_iota(jnp.int32, (SLOT, SLOT), 1)
    same = rows == cols
    turned = rows + cols == SLOT - 1
    turn = jnp.where(turned, 1.0, 0.0).astype(BF)

    def column_of(row, where):
        return jnp.sum(jnp.where(where, row, 0.0), axis=1, keepdims=True)

    def merged_ids(first, second):
        col = column_of(idb[first][:1].astype(F32), same)
        back = column_of(idb[second][:1].astype(F32), turned)
        return col, jnp.where(col >= 0.0, col, back)

    def key_ids(first, second):
        live, ids = merged_ids(first, second)
        return live, jnp.sum(jnp.where(same, ids, 0.0), axis=0, keepdims=True)

    lives, id_rows = [], []
    for g in range(4):
        for j in range(2):
            live, row = key_ids(4 * g + j, 4 * g + j + 2)
            lives.append(live)
            id_rows.append(row)
    chosen_len = len_ref[:1, :1].astype(F32)
    rejected_len = len_ref[:1, 1:2].astype(F32)
    firsts = (y % 2, (y + 1) % 2)
    for n in range(2):
        _, ids = merged_ids(firsts[n], firsts[n] + 2)
        lowest = jnp.where(ids >= chosen_len, chosen_len, 0.0)
        qid[n] = jnp.broadcast_to(ids, (SLOT, HD))
        for m in range(8):
            visible = (id_rows[m] <= ids) & (id_rows[m] >= lowest)
            bias[n, :, m * SLOT : (m + 1) * SLOT] = jnp.where(visible, HIGH, LOW)

    for dy in (1, 3):
        kv_copies[dy].wait_recv()
        forward(dy)
    q_copies[2].start()
    kv_copies[2].wait_recv()
    forward(2)
    q_copies[1].start()
    q_copies[3].start()

    def load_queries(n):
        first = firsts[n]
        live = qid[n]
        col = column_of(idb[first][:1].astype(F32), same)
        back = dot(turn, qin[first + 2])
        del live
        for h in range(GROUP):
            at = slice(h * HD, (h + 1) * HD)
            x = jnp.where(col >= 0.0, qin[first, :, at].astype(F32), back[:, at]) * SCALE
            high = x.astype(BF)
            qs[n, at, :HD] = high
            qs[n, at, HD:] = (x - high.astype(F32)).astype(BF)

    def twice(k):
        return jnp.concatenate([k, k], axis=1)

    def with_ones(v):
        return jnp.concatenate([v, jnp.ones_like(v)], axis=1)

    def prompt(group, at):
        return kv[pl.ds(group * 4, 8), pl.ds(at, PKEYS), :].reshape(8 * PKEYS, HD)

    HALF = 2 * HD

    def scores(n, i, keys):
        q = [qs[n, pl.ds(i * 2 * HALF + j * HALF, HALF), :] for j in range(2)]
        return [[dot_t(x, k) for k in keys] for x in q]

    def masked(n, s):
        limit = bias[n]
        return jnp.minimum(s, jnp.concatenate([limit, limit], axis=0))

    def highest(parts):
        tops = [jnp.max(s, axis=1, keepdims=True) for s in parts]
        return functools.reduce(jnp.maximum, tops)

    def weigh(parts, high, values):
        return sum(
            dot(jnp.exp2(s - high).astype(BF), v) for s, v in zip(parts, values)
        )

    def finish(n, i, j, result):
        out = (result[:, :HD] / result[:, HD:]).astype(BF)
        for h in range(2):
            head = 2 * j + h
            x = out[h * HD : (h + 1) * HD]
            osend[n, i, :, head * HD : (head + 1) * HD] = x
            weights = probe_ref[pl.ds(y * GROUP + i * 4 + head, 1), :]
            score[n] = score[n] + x.astype(F32) * weights

    score[...] = jnp.zeros_like(score)

    own_q.wait()
    q_copies[2].wait_recv()
    load_queries(0)
    for dy in range(NY):
        c_copies[dy].wait_recv()

    def near(i, carry):
        keys, values = [twice(prompt(0, 0))], [with_ones(prompt(0, PKEYS))]
        for j, parts in enumerate(scores(0, i, keys)):
            high = highest(parts)
            at = pl.ds(i * 2 * HALF + j * HALF, HALF)
            top[at, :] = jnp.broadcast_to(high, (HALF, HD))
            acc[at, :] = weigh(parts, high, values)
        return carry

    lax.fori_loop(0, 2, near, 0)

    for dy in (0, 1, 3, 2):
        at = 8 + (y - dy + NY) % NY
        z_copies[dy].wait_recv()
        zc_copies[dy] = remote(
            kv.at[at], kv.at[4 + at], zc_send.at[dy], zc_recv.at[dy], device(0, 0, 1)
        )
        zc_copies[dy].start()
    for dy in range(NY):
        zc_copies[dy].wait_recv()

    for g in range(4):
        for j in range(2):
            m = 2 * g + j
            live = lives[m] >= 0.0
            tail = slice(2 * PKEYS, 2 * PKEYS + 2 * SLOT)
            one = kv[4 * g + j, tail, :].astype(F32)
            two = kv[4 * g + j + 2, tail, :]
            at = slice(m * SLOT, (m + 1) * SLOT)
            krm[at, :] = jnp.where(live, one[:SLOT], dot(turn, two[:SLOT])).astype(BF)
            vrm[at, :] = jnp.where(live, one[SLOT:], dot(turn, two[SLOT:])).astype(BF)

    def out_copies(n, i):
        copies = []
        for k, dy in enumerate(((2,), (1, 3))[n]):
            copies.append(
                remote(
                    osend.at[n, i], oin.at[y, i],
                    o_send.at[dy, i], o_recv.at[dy, i], device(dy, 0, 0),
                )
            )
        return copies

    def far(i, carry):
        keys = [twice(prompt(2, 0)), twice(krm[...])]
        values = [with_ones(prompt(2, PKEYS)), with_ones(vrm[...])]
        for j, parts in enumerate(scores(0, i, keys)):
            parts = [parts[0], masked(0, parts[1])]
            at = pl.ds(i * 2 * HALF + j * HALF, HALF)
            before = top[at, :]
            high = jnp.maximum(before, highest(parts))
            factor = jnp.exp2(before - high)
            result = weigh(parts, high[:, :1], values)
            total = acc[at, :] * jnp.concatenate([factor, factor], axis=1) + result
            finish(0, i, j, total)
        for copy in out_copies(0, i):
            copy.start()
        return carry

    lax.fori_loop(0, 2, far, 0)

    q_copies[1].wait_recv()
    q_copies[3].wait_recv()
    load_queries(1)

    def whole(i, carry):
        keys = [twice(prompt(0, 0)), twice(prompt(2, 0)), twice(krm[...])]
        values = [with_ones(prompt(0, PKEYS)), with_ones(prompt(2, PKEYS)), with_ones(vrm[...])]
        for j, parts in enumerate(scores(1, i, keys)):
            parts = [parts[0], parts[1], masked(1, parts[2])]
            finish(1, i, j, weigh(parts, highest(parts), values))
        for copy in out_copies(1, i):
            copy.start()
        return carry

    lax.fori_loop(0, 2, whole, 0)

    chosen = jnp.zeros((1, 1), F32)
    rejected = jnp.zeros((1, 1), F32)

    def total_of(x):
        return jnp.sum(jnp.sum(x, axis=1, keepdims=True), axis=0, keepdims=True)

    for n in range(2):
        first = qid[n] < chosen_len
        chosen = chosen + total_of(jnp.where(first, score[n], 0.0))
        rejected = rejected + total_of(jnp.where(first, 0.0, score[n]))
    lane = lax.broadcasted_iota(jnp.int32, (8, HD), 1)
    part[blk] = jnp.where(lane == 0, chosen, jnp.where(lane == 1, rejected, 0.0))
    p_copies = []
    for i, (dy, dz, dc) in enumerate(others):
        copy = remote(
            part.at[blk], part.at[blk], p_send.at[i], p_recv.at[i], device(dy, dz, dc)
        )
        copy.start()
        p_copies.append(copy)
    for copy in p_copies:
        copy.wait_recv()
    sums = part[0]
    for i in range(1, NBLK):
        sums = sums + part[i]
    margin = sums[:1, :1] / chosen_len - sums[:1, 1:2] / rejected_len
    x = -4.0 * margin
    value = jnp.maximum(x, 0.0) + jnp.log1p(jnp.exp(-jnp.abs(x)))
    term[pair] = jnp.broadcast_to(value, (8, HD))
    t_copies = []
    for d in range(1, n_pair):
        copy = remote(
            term.at[pair], term.at[pair], t_send.at[d - 1], t_recv.at[d - 1],
            ((pair + d) % n_pair, blk),
        )
        copy.start()
        t_copies.append(copy)

    live = column_of(idb[y][:1].astype(F32), same) >= 0.0
    back = y >= 2
    take = jnp.where(back, SLOT - 1 - rows, rows) == cols
    place = jnp.where(live & take, 1.0, 0.0).astype(BF)

    def put(head, i, x):
        at = pl.ds(pl.multiple_of(head * WIDE + i * (WIDE // 2), WIDE // 2), WIDE // 2)
        att_ref[:, at] = dot(place, x).astype(BF)

    for i in range(2):
        put(y, i, osend[0, i])
    for n, dys in enumerate(((2,), (1, 3))):
        for i in range(2):
            for copy, dy in zip(out_copies(n, i), dys):
                copy.wait_recv()
                source = (y - dy + NY) % NY
                put(source, i, oin[source, i])

    for copy in t_copies:
        copy.wait_recv()
    loss = term[0]
    for i in range(1, n_pair):
        loss = loss + term[i]
    loss_ref[...] = loss[:1, :1]

    for dy in (1, 2, 3):
        kv_copies[dy].wait_send()
        q_copies[dy].wait_send()
    for dy in range(NY):
        z_copies[dy].wait_send()
        c_copies[dy].wait_send()
        zc_copies[dy].wait_send()
    for n in range(2):
        for i in range(2):
            for copy in out_copies(n, i):
                copy.wait_send()
    for copy in id_copies + p_copies + t_copies:
        copy.wait_send()


def local(n_pair, queries, prompt_keys, prompt_values, resp_keys, resp_values, slot_row, lengths, probe):
    vmem = pl.BlockSpec(memory_space=pltpu.VMEM)
    anywhere = pl.BlockSpec(memory_space=pl.ANY)
    sems = pltpu.SemaphoreType.DMA
    attended, loss = pl.pallas_call(
        functools.partial(kernel, n_pair),
        out_shape=(
            jax.ShapeDtypeStruct((SLOT, QH * HD), BF),
            jax.ShapeDtypeStruct((1, 1), F32),
        ),
        in_specs=[anywhere] * 5 + [vmem] * 3,
        out_specs=(vmem, vmem),
        scratch_shapes=[
            pltpu.VMEM((NBLK, 2 * PKEYS + 2 * SLOT, HD), BF),
            pltpu.VMEM((NBLK, 8, SLOT), jnp.int32),
            pltpu.VMEM((NY, SLOT, WIDE), BF),
            pltpu.VMEM((2, WIDE, 2 * HD), BF),
            pltpu.VMEM((8 * SLOT, HD), BF),
            pltpu.VMEM((8 * SLOT, HD), BF),
            pltpu.VMEM((2, SLOT, 8 * SLOT), F32),
            pltpu.VMEM((2, SLOT, HD), F32),
            pltpu.VMEM((WIDE, HD), F32),
            pltpu.VMEM((WIDE, 2 * HD), F32),
            pltpu.VMEM((2, SLOT, HD), F32),
            pltpu.VMEM((2, 2, SLOT, WIDE // 2), BF),
            pltpu.VMEM((NY, 2, SLOT, WIDE // 2), BF),
            pltpu.VMEM((NBLK, 8, HD), F32),
            pltpu.VMEM((n_pair, 8, HD), F32),
            sems((5,)),
            sems((NY,)), sems((NY,)),
            sems((NY,)), sems((NY,)),
            sems((NY,)), sems((NY,)),
            sems((NY,)), sems((NY,)),
            sems((NBLK - 1,)), sems((NBLK - 1,)),
            sems((NY,)), sems((NY,)),
            sems((NY, 2)), sems((NY, 2)),
            sems((NBLK - 1,)), sems((NBLK - 1,)),
            sems((8,)), sems((8,)),
        ],
        compiler_params=pltpu.CompilerParams(
            collective_id=0, has_side_effects=True, vmem_limit_bytes=56 * 2**20
        ),
        cost_estimate=pl.CostEstimate(
            flops=5_400_000_000, bytes_accessed=4_000_000, transcendentals=10_500_000
        ),
    )(
        queries[0], prompt_keys[0], prompt_values[0], resp_keys[0], resp_values[0],
        slot_row, lengths, probe.reshape(QH, HD),
    )
    return attended[None], loss[0, 0]


def solution(mesh):
    return jax.shard_map(
        functools.partial(local, mesh.shape["pair"]),
        mesh=mesh,
        in_specs=(
            P("pair", "blk", None),
            P("pair", "blk", None),
            P("pair", "blk", None),
            P("pair", "blk", None),
            P("pair", "blk", None),
            P("pair", "blk"),
            P("pair", None),
            P(),
        ),
        out_specs=(P("pair", "blk", None), P()),
        check_vma=False,
    )
```

```python
import functools

import jax
import jax.numpy as jnp
from jax import lax
from jax.experimental import pallas as pl
from jax.experimental.pallas import tpu as pltpu
from jax.sharding import PartitionSpec as P

QH = 32
KVH = 4
HD = 128
GROUP = QH // KVH
SLOT = 128
PKEYS = 256
NY = 4
NBLK = 16
PAIRS = 8
IDS = 16
BLOCK = 2 * PKEYS + 2 * SLOT
WIDE = GROUP * HD
SCALE = 1.4426950408889634 / HD**0.5
MESH = pl.DeviceIdType.MESH
BF = jnp.bfloat16
F32 = jnp.float32
LOW = -1e30
HIGH = 3e38


def dot_t(a, b):
    return lax.dot_general(a, b, (((1,), (1,)), ((), ())), preferred_element_type=F32)


def dot(a, b):
    return jnp.dot(a, b, preferred_element_type=F32)


def kernel(
    q_hbm, kp_hbm, vp_hbm, kr_hbm, vr_hbm, slot_ref, len_ref, probe_ref,
    att_ref, loss_ref,
    kv, own_ids, qin, qs, krm, vrm, bias, qid, top, acc, score, osend, oin, part, whole_sums,
    local_sem, kv_send, kv_recv, z_send, z_recv, c_send, c_recv, zc_send, zc_recv,
    q_send, q_recv, o_send, o_recv, p_send, p_recv, t_send, t_recv,
):
    pair = lax.axis_index("pair")
    blk = lax.axis_index("blk")
    y, z, c = blk // 4, (blk // 2) % 2, blk % 2
    x, z4 = pair % 4, pair // 4 * 2 + z

    def device(dy, dz, dc):
        return (pair, ((y + dy) % NY) * 4 + ((z + dz) % 2) * 2 + (c + dc) % 2)

    def across(dx, dy, dz4, dc):
        to = (z4 + dz4) % 4
        return (
            to // 2 * 4 + (x + dx) % 4,
            ((y + dy) % NY) * 4 + (to % 2) * 2 + (c + dc) % 2,
        )

    column = [(0, 0, dz4, dc) for dz4 in range(4) for dc in range(2)][1:]
    plane = [(dx, dy, 0, 0) for dx in range(4) for dy in range(NY)][1:]

    def remote(src, dst, send, recv, target):
        return pltpu.make_async_remote_copy(
            src_ref=src, dst_ref=dst, send_sem=send, recv_sem=recv,
            device_id=target, device_id_type=MESH,
        )

    def columns(head, width):
        return pl.ds(pl.multiple_of(head * width, width), width)

    def kv_parts(head, slot):
        cols = columns(head, HD)
        return (
            (kp_hbm.at[:, cols], kv.at[slot, pl.ds(0, PKEYS)]),
            (vp_hbm.at[:, cols], kv.at[slot, pl.ds(PKEYS, PKEYS)]),
            (kr_hbm.at[:, cols], kv.at[slot, pl.ds(2 * PKEYS, SLOT)]),
            (vr_hbm.at[:, cols], kv.at[slot, pl.ds(2 * PKEYS + SLOT, SLOT)]),
        )

    own = [pltpu.make_async_copy(s, d, local_sem.at[i]) for i, (s, d) in enumerate(kv_parts(y, y))]
    own_q = pltpu.make_async_copy(q_hbm.at[:, columns(y, WIDE)], qin.at[y], local_sem.at[4])
    for copy in own:
        copy.start()
    own_q.start()
    shifted = jnp.broadcast_to(slot_ref[...] + 32, (IDS, SLOT))
    upper = lax.broadcasted_iota(jnp.int32, (IDS, SLOT), 0) < IDS // 2
    coded = jnp.where(upper, shifted >> 5, shifted & 31).astype(F32).astype(BF)
    own_ids[...] = coded
    kv[y, BLOCK:, :] = coded

    barrier = pltpu.get_barrier_semaphore()
    for step in column + plane:
        pl.semaphore_signal(barrier, inc=1, device_id=across(*step), device_id_type=MESH)
    pl.semaphore_wait(barrier, len(column) + len(plane))

    kv_copies = {}
    for dy in (1, 3, 2):
        to = device(dy, 0, 0)
        parts = kv_parts((y + dy) % NY, y) + ((own_ids, kv.at[y, pl.ds(BLOCK, IDS)]),)
        for s, d in parts:
            remote(s, d, kv_send.at[dy], kv_recv.at[dy], to).start()
        kv_copies[dy] = remote(kv.at[y], kv.at[y], kv_send.at[dy], kv_recv.at[dy], to)
    q_copies = {}
    for dy in (2, 1, 3):
        q_copies[dy] = remote(
            q_hbm.at[:, columns((y + dy) % NY, WIDE)], qin.at[y],
            q_send.at[dy], q_recv.at[dy], device(dy, 0, 0),
        )
    q_copies[2].start()

    z_copies, c_copies, zc_copies = {}, {}, {}

    def forward(dy):
        at = (y - dy + NY) % NY
        z_copies[dy] = remote(
            kv.at[at], kv.at[8 + at], z_send.at[dy], z_recv.at[dy], device(0, 1, 0)
        )
        c_copies[dy] = remote(
            kv.at[at], kv.at[4 + at], c_send.at[dy], c_recv.at[dy], device(0, 0, 1)
        )
        z_copies[dy].start()
        c_copies[dy].start()

    for copy in own:
        copy.wait()
    forward(0)

    for dy in (1, 3):
        kv_copies[dy].wait_recv()
        forward(dy)
    q_copies[1].start()
    q_copies[3].start()
    kv_copies[2].wait_recv()
    forward(2)

    rows = lax.broadcasted_iota(jnp.int32, (SLOT, SLOT), 0)
    cols = lax.broadcasted_iota(jnp.int32, (SLOT, SLOT), 1)
    eye = jnp.where(rows == cols, 1.0, 0.0).astype(BF)
    turn = jnp.where(rows + cols == SLOT - 1, 1.0, 0.0).astype(BF)
    half_ids = IDS // 2

    def ids_in(slot):
        return kv[slot, BLOCK:, :]

    def column_ids(slot, order):
        t = dot_t(order, ids_in(slot))
        return 32.0 * t[:, :1] + t[:, half_ids : half_ids + 1] - 32.0

    def row_ids(t):
        return 32.0 * t[:1] + t[half_ids : half_ids + 1] - 32.0

    def merged_column(first):
        col = column_ids(first, eye)
        return jnp.where(col >= 0.0, col, column_ids(first + 2, turn))

    def merged_row(first):
        row = row_ids(ids_in(first).astype(F32))
        return jnp.where(row >= 0.0, row, row_ids(dot(ids_in(first + 2), turn)))

    firsts = (y % 2, (y + 1) % 2)

    def load_queries(n):
        first = firsts[n]
        live = column_ids(first, eye) >= 0.0
        back = dot(turn, qin[first + 2])
        for h in range(GROUP):
            at = slice(h * HD, (h + 1) * HD)
            x = jnp.where(live, qin[first, :, at].astype(F32), back[:, at]) * SCALE
            high = x.astype(BF)
            qs[n, at, :HD] = high
            qs[n, at, HD:] = (x - high.astype(F32)).astype(BF)

    def twice(k):
        return jnp.concatenate([k, k], axis=1)

    def with_ones(v):
        return jnp.concatenate([v, jnp.ones_like(v)], axis=1)

    def prompt(group, at):
        return kv[pl.ds(group * 4, 8), pl.ds(at, PKEYS), :].reshape(8 * PKEYS, HD)

    HALF = 2 * HD

    def scores(n, i, keys):
        q = [qs[n, pl.ds(i * 2 * HALF + j * HALF, HALF), :] for j in range(2)]
        return [[dot_t(x, k) for k in keys] for x in q]

    def masked(n, s):
        limit = bias[n]
        return jnp.minimum(s, jnp.concatenate([limit, limit], axis=0))

    def highest(parts):
        tops = [jnp.max(s, axis=1, keepdims=True) for s in parts]
        return functools.reduce(jnp.maximum, tops)

    def weigh(parts, high, values):
        return sum(
            dot(jnp.exp2(s - high).astype(BF), v) for s, v in zip(parts, values)
        )

    def finish(n, i, j, result):
        out = (result[:, :HD] / result[:, HD:]).astype(BF)
        for h in range(2):
            head = 2 * j + h
            x = out[h * HD : (h + 1) * HD]
            osend[n, i, :, head * HD : (head + 1) * HD] = x
            weights = probe_ref[pl.ds(y * GROUP + i * 4 + head, 1), :]
            score[n] = score[n] + x.astype(F32) * weights

    score[...] = jnp.zeros_like(score)

    own_q.wait()
    q_copies[2].wait_recv()
    load_queries(0)
    for dy in range(NY):
        c_copies[dy].wait_recv()

    def near(i, carry):
        keys, values = [twice(prompt(0, 0))], [with_ones(prompt(0, PKEYS))]
        for j, parts in enumerate(scores(0, i, keys)):
            high = highest(parts)
            at = pl.ds(i * 2 * HALF + j * HALF, HALF)
            top[at, :] = jnp.broadcast_to(high, (HALF, HD))
            acc[at, :] = weigh(parts, high, values)
        return carry

    lax.fori_loop(0, 2, near, 0)

    for dy in (0, 1, 3, 2):
        at = 8 + (y - dy + NY) % NY
        z_copies[dy].wait_recv()
        zc_copies[dy] = remote(
            kv.at[at], kv.at[4 + at], zc_send.at[dy], zc_recv.at[dy], device(0, 0, 1)
        )
        zc_copies[dy].start()
    for dy in range(NY):
        zc_copies[dy].wait_recv()

    id_rows = [merged_row(4 * g + j) for g in range(4) for j in range(2)]
    chosen_len = len_ref[:1, :1].astype(F32)
    rejected_len = len_ref[:1, 1:2].astype(F32)
    for n in range(2):
        ids = merged_column(firsts[n])
        lowest = jnp.where(ids >= chosen_len, chosen_len, 0.0)
        qid[n] = jnp.broadcast_to(ids, (SLOT, HD))
        for m in range(8):
            visible = (id_rows[m] <= ids) & (id_rows[m] >= lowest)
            bias[n, :, m * SLOT : (m + 1) * SLOT] = jnp.where(visible, HIGH, LOW)

    for g in range(4):
        for j in range(2):
            m = 2 * g + j
            live = column_ids(4 * g + j, eye) >= 0.0
            tail = slice(2 * PKEYS, BLOCK)
            one = kv[4 * g + j, tail, :].astype(F32)
            two = kv[4 * g + j + 2, tail, :]
            at = slice(m * SLOT, (m + 1) * SLOT)
            krm[at, :] = jnp.where(live, one[:SLOT], dot(turn, two[:SLOT])).astype(BF)
            vrm[at, :] = jnp.where(live, one[SLOT:], dot(turn, two[SLOT:])).astype(BF)

    def out_copies(n, i):
        copies = []
        for k, dy in enumerate(((2,), (1, 3))[n]):
            copies.append(
                remote(
                    osend.at[n, i], oin.at[y, i],
                    o_send.at[dy, i], o_recv.at[dy, i], device(dy, 0, 0),
                )
            )
        return copies

    def far(i, carry):
        keys = [twice(prompt(2, 0)), twice(krm[...])]
        values = [with_ones(prompt(2, PKEYS)), with_ones(vrm[...])]
        for j, parts in enumerate(scores(0, i, keys)):
            parts = [parts[0], masked(0, parts[1])]
            at = pl.ds(i * 2 * HALF + j * HALF, HALF)
            before = top[at, :]
            high = jnp.maximum(before, highest(parts))
            factor = jnp.exp2(before - high)
            result = weigh(parts, high[:, :1], values)
            total = acc[at, :] * jnp.concatenate([factor, factor], axis=1) + result
            finish(0, i, j, total)
        for copy in out_copies(0, i):
            copy.start()
        return carry

    lax.fori_loop(0, 2, far, 0)

    q_copies[1].wait_recv()
    q_copies[3].wait_recv()
    load_queries(1)

    def whole(i, carry):
        keys = [twice(prompt(0, 0)), twice(prompt(2, 0)), twice(krm[...])]
        values = [with_ones(prompt(0, PKEYS)), with_ones(prompt(2, PKEYS)), with_ones(vrm[...])]
        for j, parts in enumerate(scores(1, i, keys)):
            parts = [parts[0], parts[1], masked(1, parts[2])]
            finish(1, i, j, weigh(parts, highest(parts), values))
        for copy in out_copies(1, i):
            copy.start()
        return carry

    lax.fori_loop(0, 2, whole, 0)

    chosen = jnp.zeros((1, 1), F32)
    rejected = jnp.zeros((1, 1), F32)

    def total_of(x):
        return jnp.sum(jnp.sum(x, axis=1, keepdims=True), axis=0, keepdims=True)

    for n in range(2):
        first = qid[n] < chosen_len
        chosen = chosen + total_of(jnp.where(first, score[n], 0.0))
        rejected = rejected + total_of(jnp.where(first, 0.0, score[n]))
    lane = lax.broadcasted_iota(jnp.int32, (PAIRS, HD), 1)
    mine = lax.broadcasted_iota(jnp.int32, (PAIRS, HD), 0) == pair
    tile = jnp.where(lane == 0, chosen / chosen_len, rejected / rejected_len)
    z_place = z4 * 2 + c
    part[z_place] = jnp.where(mine & (lane < 2), tile, 0.0)
    p_copies = []
    for i, step in enumerate(column):
        copy = remote(
            part.at[z_place], part.at[z_place], p_send.at[i], p_recv.at[i], across(*step)
        )
        copy.start()
        p_copies.append(copy)
    for copy in p_copies:
        copy.wait_recv()
    sums = part[0]
    for i in range(1, 8):
        sums = sums + part[i]
    place_xy = x * NY + y
    whole_sums[place_xy] = sums
    t_copies = []
    for i, step in enumerate(plane):
        copy = remote(
            whole_sums.at[place_xy], whole_sums.at[place_xy], t_send.at[i], t_recv.at[i], across(*step)
        )
        copy.start()
        t_copies.append(copy)

    live = column_ids(y, eye) >= 0.0
    back = y >= 2
    take = jnp.where(back, SLOT - 1 - rows, rows) == cols
    place = jnp.where(live & take, 1.0, 0.0).astype(BF)

    def put(head, i, x):
        at = pl.ds(pl.multiple_of(head * WIDE + i * (WIDE // 2), WIDE // 2), WIDE // 2)
        att_ref[:, at] = dot(place, x).astype(BF)

    for i in range(2):
        put(y, i, osend[0, i])
    for n, dys in enumerate(((2,), (1, 3))):
        for i in range(2):
            for copy, dy in zip(out_copies(n, i), dys):
                copy.wait_recv()
                source = (y - dy + NY) % NY
                put(source, i, oin[source, i])

    for copy in t_copies:
        copy.wait_recv()
    sums = whole_sums[0]
    for i in range(1, 16):
        sums = sums + whole_sums[i]
    value = -4.0 * (sums[:, :1] - sums[:, 1:2])
    terms = jnp.maximum(value, 0.0) + jnp.log1p(jnp.exp(-jnp.abs(value)))
    loss_ref[...] = jnp.sum(terms, axis=0, keepdims=True)

    for dy in (1, 2, 3):
        kv_copies[dy].wait_send()
        q_copies[dy].wait_send()
    for dy in range(NY):
        z_copies[dy].wait_send()
        c_copies[dy].wait_send()
        zc_copies[dy].wait_send()
    for n in range(2):
        for i in range(2):
            for copy in out_copies(n, i):
                copy.wait_send()
    for copy in p_copies + t_copies:
        copy.wait_send()


def local(queries, prompt_keys, prompt_values, resp_keys, resp_values, slot_row, lengths, probe):
    vmem = pl.BlockSpec(memory_space=pltpu.VMEM)
    anywhere = pl.BlockSpec(memory_space=pl.ANY)
    sems = pltpu.SemaphoreType.DMA
    attended, loss = pl.pallas_call(
        kernel,
        out_shape=(
            jax.ShapeDtypeStruct((SLOT, QH * HD), BF),
            jax.ShapeDtypeStruct((1, 1), F32),
        ),
        in_specs=[anywhere] * 5 + [vmem] * 3,
        out_specs=(vmem, vmem),
        scratch_shapes=[
            pltpu.VMEM((NBLK, BLOCK + IDS, HD), BF),
            pltpu.VMEM((IDS, SLOT), BF),
            pltpu.VMEM((NY, SLOT, WIDE), BF),
            pltpu.VMEM((2, WIDE, 2 * HD), BF),
            pltpu.VMEM((8 * SLOT, HD), BF),
            pltpu.VMEM((8 * SLOT, HD), BF),
            pltpu.VMEM((2, SLOT, 8 * SLOT), F32),
            pltpu.VMEM((2, SLOT, HD), F32),
            pltpu.VMEM((WIDE, HD), F32),
            pltpu.VMEM((WIDE, 2 * HD), F32),
            pltpu.VMEM((2, SLOT, HD), F32),
            pltpu.VMEM((2, 2, SLOT, WIDE // 2), BF),
            pltpu.VMEM((NY, 2, SLOT, WIDE // 2), BF),
            pltpu.VMEM((8, PAIRS, HD), F32),
            pltpu.VMEM((16, PAIRS, HD), F32),
            sems((5,)),
            sems((NY,)), sems((NY,)),
            sems((NY,)), sems((NY,)),
            sems((NY,)), sems((NY,)),
            sems((NY,)), sems((NY,)),
            sems((NY,)), sems((NY,)),
            sems((NY, 2)), sems((NY, 2)),
            sems((7,)), sems((7,)),
            sems((15,)), sems((15,)),
        ],
        compiler_params=pltpu.CompilerParams(
            collective_id=0, has_side_effects=True, vmem_limit_bytes=56 * 2**20
        ),
        cost_estimate=pl.CostEstimate(
            flops=5_400_000_000, bytes_accessed=4_000_000, transcendentals=10_500_000
        ),
    )(
        queries[0], prompt_keys[0], prompt_values[0], resp_keys[0], resp_values[0],
        slot_row, lengths, probe.reshape(QH, HD),
    )
    return attended[None], loss[0, 0]


def solution(mesh):
    return jax.shard_map(
        local,
        mesh=mesh,
        in_specs=(
            P("pair", "blk", None),
            P("pair", "blk", None),
            P("pair", "blk", None),
            P("pair", "blk", None),
            P("pair", "blk", None),
            P("pair", "blk"),
            P("pair", None),
            P(),
        ),
        out_specs=(P("pair", "blk", None), P()),
        check_vma=False,
    )
```

```python
import functools

import jax
import jax.numpy as jnp
from jax import lax
from jax.experimental import pallas as pl
from jax.experimental.pallas import tpu as pltpu
from jax.sharding import PartitionSpec as P

QH = 32
KVH = 4
HD = 128
GROUP = QH // KVH
SLOT = 128
PKEYS = 256
NY = 4
NBLK = 16
PAIRS = 8
IDS = 16
RESP = 2 * SLOT
WIDE = GROUP * HD
SCALE = 1.4426950408889634 / HD**0.5
MESH = pl.DeviceIdType.MESH
BF = jnp.bfloat16
F32 = jnp.float32
LOW = -1e30
HIGH = 3e38


def dot_t(a, b):
    return lax.dot_general(a, b, (((1,), (1,)), ((), ())), preferred_element_type=F32)


def dot(a, b):
    return jnp.dot(a, b, preferred_element_type=F32)


def kernel(
    q_hbm, kp_hbm, vp_hbm, kr_hbm, vr_hbm, slot_hbm, len_hbm, probe_hbm,
    att_hbm, loss_ref,
    slot_ref, len_ref, probe_ref, att, kv, resp, merged, ids, qin, qs, bias, qid, top, acc, score, osend, oin, part, whole_sums,
    local_sem, small_sem, att_sem, kv_send, kv_recv, r_send, r_recv, id_send, id_recv, z_send, z_recv, c_send, c_recv, zc_send, zc_recv,
    q_send, q_recv, o_send, o_recv, p_send, p_recv, t_send, t_recv,
):
    pair = lax.axis_index("pair")
    blk = lax.axis_index("blk")
    y, z, c = blk // 4, (blk // 2) % 2, blk % 2
    x, z4 = pair % 4, pair // 4 * 2 + z

    def device(dy, dz, dc):
        return (pair, ((y + dy) % NY) * 4 + ((z + dz) % 2) * 2 + (c + dc) % 2)

    def across(dx, dy, dz4, dc):
        to = (z4 + dz4) % 4
        return (
            to // 2 * 4 + (x + dx) % 4,
            ((y + dy) % NY) * 4 + (to % 2) * 2 + (c + dc) % 2,
        )

    column = [(0, 0, dz4, dc) for dz4 in range(4) for dc in range(2)][1:]
    plane = [(dx, dy, 0, 0) for dx in range(4) for dy in range(NY)][1:]

    def remote(src, dst, send, recv, target):
        return pltpu.make_async_remote_copy(
            src_ref=src, dst_ref=dst, send_sem=send, recv_sem=recv,
            device_id=target, device_id_type=MESH,
        )

    def columns(head, width):
        return pl.ds(pl.multiple_of(head * width, width), width)

    def prompt_parts(head):
        cols = columns(head, HD)
        return (
            (kp_hbm.at[:, cols], kv.at[0, y, pl.ds(0, PKEYS)]),
            (vp_hbm.at[:, cols], kv.at[0, y, pl.ds(PKEYS, PKEYS)]),
        )

    def resp_parts(head):
        cols = columns(head, HD)
        return (
            (kr_hbm.at[:, cols], resp.at[y, pl.ds(0, SLOT)]),
            (vr_hbm.at[:, cols], resp.at[y, pl.ds(SLOT, SLOT)]),
        )

    own = [
        pltpu.make_async_copy(s, d, local_sem.at[i])
        for i, (s, d) in enumerate(prompt_parts(y) + resp_parts(y))
    ]
    own_q = [
        pltpu.make_async_copy(
            q_hbm.at[:, columns(y * 2 + i, WIDE // 2)], qin.at[y, i], local_sem.at[4 + i]
        )
        for i in range(2)
    ]
    for copy in own + own_q:
        copy.start()
    small = [
        pltpu.make_async_copy(s, d, small_sem.at[i])
        for i, (s, d) in enumerate(
            ((slot_hbm, slot_ref), (len_hbm, len_ref), (probe_hbm, probe_ref))
        )
    ]
    for copy in small:
        copy.start()

    small[0].wait()
    shifted = jnp.broadcast_to(slot_ref[...] + 32, (IDS, SLOT))
    upper = lax.broadcasted_iota(jnp.int32, (IDS, SLOT), 0) < IDS // 2
    ids[y] = jnp.where(upper, shifted >> 5, shifted & 31).astype(F32).astype(BF)

    barrier = pltpu.get_barrier_semaphore()
    for step in column + plane:
        pl.semaphore_signal(barrier, inc=1, device_id=across(*step), device_id_type=MESH)
    pl.semaphore_wait(barrier, len(column) + len(plane))

    kv_copies, r_copies, q_copies = {}, {}, {}

    def send_prompt(dy):
        to = device(dy, 0, 0)
        for s, d in prompt_parts((y + dy) % NY):
            remote(s, d, kv_send.at[dy], kv_recv.at[dy], to).start()
        kv_copies[dy] = remote(kv.at[0, y], kv.at[0, y], kv_send.at[dy], kv_recv.at[dy], to)

    def send_resp(dy):
        to = device(dy, 0, 0)
        for s, d in resp_parts((y + dy) % NY):
            remote(s, d, r_send.at[dy], r_recv.at[dy], to).start()
        r_copies[dy] = remote(resp.at[y], resp.at[y], r_send.at[dy], r_recv.at[dy], to)

    for dy in (1, 2, 3):
        for i in range(2):
            q_copies[dy, i] = remote(
                q_hbm.at[:, columns(((y + dy) % NY) * 2 + i, WIDE // 2)], qin.at[y, i],
                q_send.at[dy, i], q_recv.at[dy, i], device(dy, 0, 0),
            )

    def send_queries(dy, i):
        q_copies[dy, i].start()

    id_copies = {
        dy: remote(ids.at[y], ids.at[y], id_send.at[dy], id_recv.at[dy], device(dy, 0, 0))
        for dy in (1, 2, 3)
    }
    send_prompt(1)
    send_prompt(3)
    for dy in (1, 2, 3):
        id_copies[dy].start()

    z_copies, c_copies, zc_copies = {}, {}, {}

    def pass_on(name, piece):
        z_copies[name] = remote(
            piece(0), piece(2), z_send.at[name], z_recv.at[name], device(0, 1, 0)
        )
        c_copies[name] = remote(
            piece(0), piece(1), c_send.at[name], c_recv.at[name], device(0, 0, 1)
        )
        zc_copies[name] = remote(
            piece(2), piece(3), zc_send.at[name], zc_recv.at[name], device(0, 0, 1)
        )

    def start_on(name):
        z_copies[name].start()
        c_copies[name].start()

    def forward(dy):
        at = (y - dy + NY) % NY
        pass_on(dy, lambda group: kv.at[group, at])
        start_on(dy)

    for copy in own:
        copy.wait()
    forward(0)

    c_copies[0].wait_recv()
    send_prompt(2)
    for dy in (1, 3):
        kv_copies[dy].wait_recv()
        forward(dy)
    send_queries(2, 0)
    kv_copies[2].wait_recv()
    forward(2)
    for dy in (1, 3, 2):
        send_resp(dy)

    rows = lax.broadcasted_iota(jnp.int32, (SLOT, SLOT), 0)
    cols = lax.broadcasted_iota(jnp.int32, (SLOT, SLOT), 1)
    eye = jnp.where(rows == cols, 1.0, 0.0).astype(BF)
    turn = jnp.where(rows + cols == SLOT - 1, 1.0, 0.0).astype(BF)
    half_ids = IDS // 2

    def column_ids(slot, order):
        t = dot_t(order, ids[slot])
        return 32.0 * t[:, :1] + t[:, half_ids : half_ids + 1] - 32.0

    def row_ids(t):
        return 32.0 * t[:1] + t[half_ids : half_ids + 1] - 32.0

    firsts = (y % 2, (y + 1) % 2)

    def load_queries(n, i):
        first = firsts[n]
        live = column_ids(first, eye) >= 0.0
        back = dot(turn, qin[first + 2, i])
        for h in range(GROUP // 2):
            at = slice(h * HD, (h + 1) * HD)
            to = slice((i * (GROUP // 2) + h) * HD, (i * (GROUP // 2) + h + 1) * HD)
            x = jnp.where(live, qin[first, i, :, at].astype(F32), back[:, at]) * SCALE
            high = x.astype(BF)
            qs[n, to, :HD] = high
            qs[n, to, HD:] = (x - high.astype(F32)).astype(BF)

    def twice(k):
        return jnp.concatenate([k, k], axis=1)

    def with_ones(v):
        return jnp.concatenate([v, jnp.ones_like(v)], axis=1)

    def prompt(groups, at):
        part = kv[groups, :, at : at + PKEYS, :]
        return part.reshape(part.shape[0] * NY * PKEYS, HD)

    def response(at):
        return merged[:, :, at : at + SLOT, :].reshape(8 * SLOT, HD)

    HALF = 2 * HD

    def scores(n, i, keys):
        q = [qs[n, pl.ds(i * 2 * HALF + j * HALF, HALF), :] for j in range(2)]
        return [dot_t(x, keys) for x in q]

    def masked(n, s):
        at = s.shape[1] - 8 * SLOT
        limit = bias[n]
        limit = jnp.concatenate([limit, limit], axis=0)
        return jnp.concatenate([s[:, :at], jnp.minimum(s[:, at:], limit)], axis=1)

    def highest(s):
        return jnp.max(s, axis=1, keepdims=True)

    def weigh(s, high, values):
        return dot(jnp.exp2(s - high).astype(BF), values)

    def finish(n, i, j, result):
        out = (result[:, :HD] / result[:, HD:]).astype(BF)
        for h in range(2):
            head = 2 * j + h
            x = out[h * HD : (h + 1) * HD]
            osend[n, i, :, head * HD : (head + 1) * HD] = x
            weights = probe_ref[pl.ds(y * GROUP + i * 4 + head, 1), :]
            score[n] = score[n] + x.astype(F32) * weights

    score[...] = jnp.zeros_like(score)

    def take_z(name):
        z_copies[name].wait_recv()
        zc_copies[name].start()

    pass_on(NY, lambda group: merged.at[group])

    def merge():
        for dy in (1, 3, 2):
            r_copies[dy].wait_recv()
        for j in range(2):
            live = column_ids(j, eye) >= 0.0
            for part_of in range(2):
                at = slice(part_of * SLOT, (part_of + 1) * SLOT)
                one = resp[j, at, :].astype(F32)
                two = dot(turn, resp[j + 2, at, :])
                merged[0, j, at, :] = jnp.where(live, one, two).astype(BF)
            one = ids[j].astype(F32)
            two = dot(ids[j + 2], turn)
            merged[0, j, RESP:, :] = jnp.where(row_ids(one) >= 0.0, one, two).astype(BF)
        start_on(NY)

    def near(k, carry):
        @pl.when(k == 0)
        def _():
            own_q[0].wait()
            q_copies[2, 0].wait_recv()
            send_queries(2, 1)
            for dy in (1, 2, 3):
                id_copies[dy].wait_recv()
            load_queries(0, 0)
            for dy in (1, 2, 3):
                c_copies[dy].wait_recv()

        @pl.when(k == 1)
        def _():
            merge()
            send_queries(1, 0)
            send_queries(3, 0)
            for name in (0, 1, 3):
                take_z(name)
            own_q[1].wait()
            q_copies[2, 1].wait_recv()
            send_queries(1, 1)
            send_queries(3, 1)
            load_queries(0, 1)

        plane = slice(0, 2)
        keys, values = twice(prompt(plane, 0)), with_ones(prompt(plane, PKEYS))
        for j, s in enumerate(scores(0, k, keys)):
            high = highest(s)
            at = pl.ds(k * 2 * HALF + j * HALF, HALF)
            top[at, :] = jnp.broadcast_to(high, (HALF, HD))
            acc[at, :] = weigh(s, high, values)
        return carry

    lax.fori_loop(0, 2, near, 0)

    for name in (2, NY):
        take_z(name)
    c_copies[NY].wait_recv()
    for name in range(NY + 1):
        zc_copies[name].wait_recv()

    id_rows = [
        row_ids(merged[g, j, RESP:, :].astype(F32)) for g in range(4) for j in range(2)
    ]
    small[1].wait()
    small[2].wait()
    chosen_len = len_ref[:1, :1].astype(F32)
    rejected_len = len_ref[:1, 1:2].astype(F32)
    for n in range(2):
        t = dot_t(eye, merged[0, firsts[n], RESP:, :])
        row_of = 32.0 * t[:, :1] + t[:, half_ids : half_ids + 1] - 32.0
        lowest = jnp.where(row_of >= chosen_len, chosen_len, 0.0)
        qid[n] = jnp.broadcast_to(row_of, (SLOT, HD))
        for m in range(8):
            visible = (id_rows[m] <= row_of) & (id_rows[m] >= lowest)
            bias[n, :, m * SLOT : (m + 1) * SLOT] = jnp.where(visible, HIGH, LOW)

    def out_copies(n, i):
        return [
            remote(
                osend.at[n, i], oin.at[y, i],
                o_send.at[dy, i], o_recv.at[dy, i], device(dy, 0, 0),
            )
            for dy in ((2,), (1, 3))[n]
        ]

    def far(i, carry):
        plane = slice(2, 4)
        keys = twice(jnp.concatenate([prompt(plane, 0), response(0)], axis=0))
        values = with_ones(jnp.concatenate([prompt(plane, PKEYS), response(SLOT)], axis=0))
        for j, s in enumerate(scores(0, i, keys)):
            s = masked(0, s)
            at = pl.ds(i * 2 * HALF + j * HALF, HALF)
            before = top[at, :]
            high = jnp.maximum(before, highest(s))
            factor = jnp.exp2(before - high)
            result = weigh(s, high[:, :1], values)
            total = acc[at, :] * jnp.concatenate([factor, factor], axis=1) + result
            finish(0, i, j, total)
        for copy in out_copies(0, i):
            copy.start()
        return carry

    lax.fori_loop(0, 2, far, 0)

    def whole(i, carry):
        for half in range(2):

            @pl.when(i == half)
            def _():
                q_copies[1, half].wait_recv()
                q_copies[3, half].wait_recv()
                load_queries(1, half)

        both = slice(0, 4)
        keys = twice(jnp.concatenate([prompt(both, 0), response(0)], axis=0))
        values = with_ones(jnp.concatenate([prompt(both, PKEYS), response(SLOT)], axis=0))
        for j, s in enumerate(scores(1, i, keys)):
            s = masked(1, s)
            finish(1, i, j, weigh(s, highest(s), values))
        for copy in out_copies(1, i):
            copy.start()
        return carry

    lax.fori_loop(0, 2, whole, 0)

    chosen = jnp.zeros((1, 1), F32)
    rejected = jnp.zeros((1, 1), F32)

    def total_of(x):
        return jnp.sum(jnp.sum(x, axis=1, keepdims=True), axis=0, keepdims=True)

    for n in range(2):
        first = qid[n] < chosen_len
        chosen = chosen + total_of(jnp.where(first, score[n], 0.0))
        rejected = rejected + total_of(jnp.where(first, 0.0, score[n]))
    lane = lax.broadcasted_iota(jnp.int32, (PAIRS, HD), 1)
    mine = lax.broadcasted_iota(jnp.int32, (PAIRS, HD), 0) == pair
    tile = jnp.where(lane == 0, chosen / chosen_len, rejected / rejected_len)
    z_place = z4 * 2 + c
    part[z_place] = jnp.where(mine & (lane < 2), tile, 0.0)
    p_copies = []
    for i, step in enumerate(column):
        copy = remote(
            part.at[z_place], part.at[z_place], p_send.at[i], p_recv.at[i], across(*step)
        )
        copy.start()
        p_copies.append(copy)
    for copy in p_copies:
        copy.wait_recv()
    sums = part[0]
    for i in range(1, 8):
        sums = sums + part[i]
    place_xy = x * NY + y
    whole_sums[place_xy] = sums
    t_copies = []
    for i, step in enumerate(plane):
        copy = remote(
            whole_sums.at[place_xy], whole_sums.at[place_xy], t_send.at[i], t_recv.at[i], across(*step)
        )
        copy.start()
        t_copies.append(copy)

    live = column_ids(y, eye) >= 0.0
    back = y >= 2
    take = jnp.where(back, SLOT - 1 - rows, rows) == cols
    place = jnp.where(live & take, 1.0, 0.0).astype(BF)

    att_copies = []

    def put(head, i, x):
        at = columns(head * 2 + i, WIDE // 2)
        k = len(att_copies)
        att[k] = dot(place, x).astype(BF)
        copy = pltpu.make_async_copy(att.at[k], att_hbm.at[:, at], att_sem.at[k])
        copy.start()
        att_copies.append(copy)

    for i in range(2):
        put(y, i, osend[0, i])
    for n, dys in enumerate(((2,), (1, 3))):
        for i in range(2):
            for copy, dy in zip(out_copies(n, i), dys):
                copy.wait_recv()
                source = (y - dy + NY) % NY
                put(source, i, oin[source, i])

    for copy in t_copies:
        copy.wait_recv()
    sums = whole_sums[0]
    for i in range(1, 16):
        sums = sums + whole_sums[i]
    value = -4.0 * (sums[:, :1] - sums[:, 1:2])
    terms = jnp.maximum(value, 0.0) + jnp.log1p(jnp.exp(-jnp.abs(value)))
    loss_ref[...] = jnp.sum(terms, axis=0, keepdims=True)

    for copy in att_copies:
        copy.wait()
    for dy in (1, 2, 3):
        kv_copies[dy].wait_send()
        r_copies[dy].wait_send()
        id_copies[dy].wait_send()
        for i in range(2):
            q_copies[dy, i].wait_send()
    for name in range(NY + 1):
        z_copies[name].wait_send()
        c_copies[name].wait_send()
        zc_copies[name].wait_send()
    for n in range(2):
        for i in range(2):
            for copy in out_copies(n, i):
                copy.wait_send()
    for copy in p_copies + t_copies:
        copy.wait_send()


def local(queries, prompt_keys, prompt_values, resp_keys, resp_values, slot_row, lengths, probe):
    vmem = pl.BlockSpec(memory_space=pltpu.VMEM)
    anywhere = pl.BlockSpec(memory_space=pl.ANY)
    sems = pltpu.SemaphoreType.DMA
    attended, loss = pl.pallas_call(
        kernel,
        out_shape=(
            jax.ShapeDtypeStruct((SLOT, QH * HD), BF),
            jax.ShapeDtypeStruct((1, 1), F32),
        ),
        in_specs=[anywhere] * 8,
        out_specs=(anywhere, vmem),
        scratch_shapes=[
            pltpu.VMEM((1, SLOT), jnp.int32),
            pltpu.VMEM((1, 2), jnp.int32),
            pltpu.VMEM((QH, HD), F32),
            pltpu.VMEM((2 * NY, SLOT, WIDE // 2), BF),
            pltpu.VMEM((4, NY, 2 * PKEYS, HD), BF),
            pltpu.VMEM((NY, RESP, HD), BF),
            pltpu.VMEM((4, 2, RESP + IDS, HD), BF),
            pltpu.VMEM((NY, IDS, SLOT), BF),
            pltpu.VMEM((NY, 2, SLOT, WIDE // 2), BF),
            pltpu.VMEM((2, WIDE, 2 * HD), BF),
            pltpu.VMEM((2, SLOT, 8 * SLOT), F32),
            pltpu.VMEM((2, SLOT, HD), F32),
            pltpu.VMEM((WIDE, HD), F32),
            pltpu.VMEM((WIDE, 2 * HD), F32),
            pltpu.VMEM((2, SLOT, HD), F32),
            pltpu.VMEM((2, 2, SLOT, WIDE // 2), BF),
            pltpu.VMEM((NY, 2, SLOT, WIDE // 2), BF),
            pltpu.VMEM((8, PAIRS, HD), F32),
            pltpu.VMEM((16, PAIRS, HD), F32),
            sems((6,)),
            sems((3,)),
            sems((2 * NY,)),
            sems((NY,)), sems((NY,)),
            sems((NY,)), sems((NY,)),
            sems((NY,)), sems((NY,)),
            sems((NY + 1,)), sems((NY + 1,)),
            sems((NY + 1,)), sems((NY + 1,)),
            sems((NY + 1,)), sems((NY + 1,)),
            sems((NY, 2)), sems((NY, 2)),
            sems((NY, 2)), sems((NY, 2)),
            sems((7,)), sems((7,)),
            sems((15,)), sems((15,)),
        ],
        compiler_params=pltpu.CompilerParams(
            collective_id=0, has_side_effects=True, vmem_limit_bytes=56 * 2**20
        ),
        cost_estimate=pl.CostEstimate(
            flops=5_400_000_000, bytes_accessed=4_000_000, transcendentals=10_500_000
        ),
    )(
        queries[0], prompt_keys[0], prompt_values[0], resp_keys[0], resp_values[0],
        slot_row, lengths, probe.reshape(QH, HD),
    )
    return attended[None], loss[0, 0]


def solution(mesh):
    return jax.shard_map(
        local,
        mesh=mesh,
        in_specs=(
            P("pair", "blk", None),
            P("pair", "blk", None),
            P("pair", "blk", None),
            P("pair", "blk", None),
            P("pair", "blk", None),
            P("pair", "blk"),
            P("pair", None),
            P(),
        ),
        out_specs=(P("pair", "blk", None), P()),
        check_vma=False,
    )
```

```python
import functools

import jax
import jax.numpy as jnp
from jax import lax
from jax.experimental import pallas as pl
from jax.experimental.pallas import tpu as pltpu
from jax.sharding import PartitionSpec as P

QH = 32
KVH = 4
HD = 128
GROUP = QH // KVH
SLOT = 128
PKEYS = 256
NY = 4
NBLK = 16
PAIRS = 8
IDS = 16
RESP = 2 * SLOT
WIDE = GROUP * HD
SCALE = 1.4426950408889634 / HD**0.5
MESH = pl.DeviceIdType.MESH
BF = jnp.bfloat16
F32 = jnp.float32
LOW = -1e30
HIGH = 3e38


def dot_t(a, b):
    return lax.dot_general(a, b, (((1,), (1,)), ((), ())), preferred_element_type=F32)


def dot(a, b):
    return jnp.dot(a, b, preferred_element_type=F32)


def kernel(
    q_hbm, kp_hbm, vp_hbm, kr_hbm, vr_hbm, slot_hbm, len_hbm, probe_hbm,
    att_hbm, loss_ref,
    slot_ref, len_ref, probe_ref, att, kv, resp, merged, ids, qin, qs, bias, qid, top, acc, score, osend, oin, part, whole_sums,
    local_sem, small_sem, att_sem, kv_send, kv_recv, r_send, r_recv, id_send, id_recv, z_send, z_recv, c_send, c_recv, zc_send, zc_recv,
    q_send, q_recv, o_send, o_recv, p_send, p_recv, t_send, t_recv,
):
    pair = lax.axis_index("pair")
    blk = lax.axis_index("blk")
    y, z, c = blk // 4, (blk // 2) % 2, blk % 2
    x, z4 = pair % 4, pair // 4 * 2 + z

    def device(dy, dz, dc):
        return (pair, ((y + dy) % NY) * 4 + ((z + dz) % 2) * 2 + (c + dc) % 2)

    def across(dx, dy, dz4, dc):
        to = (z4 + dz4) % 4
        return (
            to // 2 * 4 + (x + dx) % 4,
            ((y + dy) % NY) * 4 + (to % 2) * 2 + (c + dc) % 2,
        )

    column = [(0, 0, dz4, dc) for dz4 in range(4) for dc in range(2)][1:]
    plane = [(dx, dy, 0, 0) for dx in range(4) for dy in range(NY)][1:]

    def remote(src, dst, send, recv, target):
        return pltpu.make_async_remote_copy(
            src_ref=src, dst_ref=dst, send_sem=send, recv_sem=recv,
            device_id=target, device_id_type=MESH,
        )

    def columns(head, width):
        return pl.ds(pl.multiple_of(head * width, width), width)

    def prompt_parts(head):
        cols = columns(head, HD)
        return (
            (kp_hbm.at[:, cols], kv.at[0, y, pl.ds(0, PKEYS)]),
            (vp_hbm.at[:, cols], kv.at[0, y, pl.ds(PKEYS, PKEYS)]),
        )

    def resp_parts(head):
        cols = columns(head, HD)
        return (
            (kr_hbm.at[:, cols], resp.at[y, pl.ds(0, SLOT)]),
            (vr_hbm.at[:, cols], resp.at[y, pl.ds(SLOT, SLOT)]),
        )

    own = [
        pltpu.make_async_copy(s, d, local_sem.at[i])
        for i, (s, d) in enumerate(prompt_parts(y) + resp_parts(y))
    ]
    own_q = [
        pltpu.make_async_copy(
            q_hbm.at[:, columns(y * 2 + i, WIDE // 2)], qin.at[y, i], local_sem.at[4 + i]
        )
        for i in range(2)
    ]
    for copy in own + own_q:
        copy.start()
    small = [
        pltpu.make_async_copy(s, d, small_sem.at[i])
        for i, (s, d) in enumerate(
            ((slot_hbm, slot_ref), (len_hbm, len_ref), (probe_hbm, probe_ref))
        )
    ]
    for copy in small:
        copy.start()

    barrier = pltpu.get_barrier_semaphore()
    for step in column + plane:
        pl.semaphore_signal(barrier, inc=1, device_id=across(*step), device_id_type=MESH)
    small[0].wait()
    shifted = jnp.broadcast_to(slot_ref[...] + 32, (IDS, SLOT))
    upper = lax.broadcasted_iota(jnp.int32, (IDS, SLOT), 0) < IDS // 2
    ids[y] = jnp.where(upper, shifted >> 5, shifted & 31).astype(F32).astype(BF)
    pl.semaphore_wait(barrier, len(column) + len(plane))

    kv_copies, r_copies, q_copies = {}, {}, {}

    def send_prompt(dy):
        to = device(dy, 0, 0)
        for s, d in prompt_parts((y + dy) % NY):
            remote(s, d, kv_send.at[dy], kv_recv.at[dy], to).start()
        kv_copies[dy] = remote(kv.at[0, y], kv.at[0, y], kv_send.at[dy], kv_recv.at[dy], to)

    def send_resp(dy):
        to = device(dy, 0, 0)
        for s, d in resp_parts((y + dy) % NY):
            remote(s, d, r_send.at[dy], r_recv.at[dy], to).start()
        r_copies[dy] = remote(resp.at[y], resp.at[y], r_send.at[dy], r_recv.at[dy], to)

    for dy in (1, 2, 3):
        for i in range(2):
            q_copies[dy, i] = remote(
                q_hbm.at[:, columns(((y + dy) % NY) * 2 + i, WIDE // 2)], qin.at[y, i],
                q_send.at[dy, i], q_recv.at[dy, i], device(dy, 0, 0),
            )

    def send_queries(dy, i):
        q_copies[dy, i].start()

    id_copies = {
        dy: remote(ids.at[y], ids.at[y], id_send.at[dy], id_recv.at[dy], device(dy, 0, 0))
        for dy in (1, 2, 3)
    }
    send_prompt(1)
    send_prompt(3)
    for dy in (1, 2, 3):
        id_copies[dy].start()

    z_copies, c_copies, zc_copies = {}, {}, {}

    def pass_on(name, piece):
        z_copies[name] = remote(
            piece(0), piece(2), z_send.at[name], z_recv.at[name], device(0, 1, 0)
        )
        c_copies[name] = remote(
            piece(0), piece(1), c_send.at[name], c_recv.at[name], device(0, 0, 1)
        )
        zc_copies[name] = remote(
            piece(2), piece(3), zc_send.at[name], zc_recv.at[name], device(0, 0, 1)
        )

    def start_on(name):
        z_copies[name].start()
        c_copies[name].start()

    def forward(dy):
        at = (y - dy + NY) % NY
        pass_on(dy, lambda group: kv.at[group, at])
        start_on(dy)

    for copy in own:
        copy.wait()
    forward(0)

    c_copies[0].wait_recv()
    send_prompt(2)
    for dy in (1, 3):
        kv_copies[dy].wait_recv()
        forward(dy)
    for dy in (2, 1, 3):
        send_resp(dy)
    kv_copies[2].wait_recv()
    forward(2)
    c_copies[2].wait_recv()
    send_queries(2, 0)

    rows = lax.broadcasted_iota(jnp.int32, (SLOT, SLOT), 0)
    cols = lax.broadcasted_iota(jnp.int32, (SLOT, SLOT), 1)
    eye = jnp.where(rows == cols, 1.0, 0.0).astype(BF)
    turn = jnp.where(rows + cols == SLOT - 1, 1.0, 0.0).astype(BF)
    half_ids = IDS // 2

    def column_ids(slot, order):
        t = dot_t(order, ids[slot])
        return 32.0 * t[:, :1] + t[:, half_ids : half_ids + 1] - 32.0

    def row_ids(t):
        return 32.0 * t[:1] + t[half_ids : half_ids + 1] - 32.0

    pass_on(NY, lambda group: merged.at[group])

    for dy in (1, 2, 3):
        id_copies[dy].wait_recv()
    for dy in (1, 3, 2):
        r_copies[dy].wait_recv()
    for j in range(2):
        live = column_ids(j, eye) >= 0.0
        for part_of in range(2):
            at = slice(part_of * SLOT, (part_of + 1) * SLOT)
            one = resp[j, at, :].astype(F32)
            two = dot(turn, resp[j + 2, at, :])
            merged[0, j, at, :] = jnp.where(live, one, two).astype(BF)
        one = ids[j].astype(F32)
        two = dot(ids[j + 2], turn)
        merged[0, j, RESP:, :] = jnp.where(row_ids(one) >= 0.0, one, two).astype(BF)
    start_on(NY)
    send_queries(2, 1)

    firsts = (y % 2, (y + 1) % 2)

    def load_queries(n, i):
        first = firsts[n]
        live = column_ids(first, eye) >= 0.0
        back = dot(turn, qin[first + 2, i])
        for h in range(GROUP // 2):
            at = slice(h * HD, (h + 1) * HD)
            to = slice((i * (GROUP // 2) + h) * HD, (i * (GROUP // 2) + h + 1) * HD)
            x = jnp.where(live, qin[first, i, :, at].astype(F32), back[:, at]) * SCALE
            high = x.astype(BF)
            qs[n, to, :HD] = high
            qs[n, to, HD:] = (x - high.astype(F32)).astype(BF)

    def twice(k):
        return jnp.concatenate([k, k], axis=1)

    def with_ones(v):
        return jnp.concatenate([v, jnp.ones_like(v)], axis=1)

    def prompt(groups, at):
        part = kv[groups, :, at : at + PKEYS, :]
        return part.reshape(part.shape[0] * NY * PKEYS, HD)

    def response(at):
        return merged[:, :, at : at + SLOT, :].reshape(8 * SLOT, HD)

    HALF = 2 * HD

    def scores(n, i, keys):
        q = [qs[n, pl.ds(i * 2 * HALF + j * HALF, HALF), :] for j in range(2)]
        return [dot_t(x, keys) for x in q]

    def masked(n, s):
        at = s.shape[1] - 8 * SLOT
        limit = bias[n]
        limit = jnp.concatenate([limit, limit], axis=0)
        return jnp.concatenate([s[:, :at], jnp.minimum(s[:, at:], limit)], axis=1)

    def highest(s):
        return jnp.max(s, axis=1, keepdims=True)

    def weigh(s, high, values):
        return dot(jnp.exp2(s - high).astype(BF), values)

    def finish(n, i, j, result):
        out = (result[:, :HD] / result[:, HD:]).astype(BF)
        for h in range(2):
            head = 2 * j + h
            x = out[h * HD : (h + 1) * HD]
            osend[n, i, :, head * HD : (head + 1) * HD] = x
            weights = probe_ref[pl.ds(y * GROUP + i * 4 + head, 1), :]
            score[n] = score[n] + x.astype(F32) * weights

    score[...] = jnp.zeros_like(score)

    def take_z(name):
        z_copies[name].wait_recv()
        zc_copies[name].start()

    def near(k, carry):
        @pl.when(k == 0)
        def _():
            own_q[0].wait()
            q_copies[2, 0].wait_recv()
            send_queries(1, 0)
            send_queries(3, 0)
            load_queries(0, 0)
            for dy in (1, 3):
                c_copies[dy].wait_recv()

        @pl.when(k == 1)
        def _():
            for name in (0, 1, 3, 2, NY):
                take_z(name)
            own_q[1].wait()
            q_copies[2, 1].wait_recv()
            send_queries(1, 1)
            send_queries(3, 1)
            load_queries(0, 1)

        plane = slice(0, 2)
        keys, values = twice(prompt(plane, 0)), with_ones(prompt(plane, PKEYS))
        for j, s in enumerate(scores(0, k, keys)):
            high = highest(s)
            at = pl.ds(k * 2 * HALF + j * HALF, HALF)
            top[at, :] = jnp.broadcast_to(high, (HALF, HD))
            acc[at, :] = weigh(s, high, values)
        return carry

    lax.fori_loop(0, 2, near, 0)

    c_copies[NY].wait_recv()
    for name in range(NY + 1):
        zc_copies[name].wait_recv()

    id_rows = [
        row_ids(merged[g, j, RESP:, :].astype(F32)) for g in range(4) for j in range(2)
    ]
    small[1].wait()
    small[2].wait()
    chosen_len = len_ref[:1, :1].astype(F32)
    rejected_len = len_ref[:1, 1:2].astype(F32)
    for n in range(2):
        t = dot_t(eye, merged[0, firsts[n], RESP:, :])
        row_of = 32.0 * t[:, :1] + t[:, half_ids : half_ids + 1] - 32.0
        lowest = jnp.where(row_of >= chosen_len, chosen_len, 0.0)
        qid[n] = jnp.broadcast_to(row_of, (SLOT, HD))
        for m in range(8):
            visible = (id_rows[m] <= row_of) & (id_rows[m] >= lowest)
            bias[n, :, m * SLOT : (m + 1) * SLOT] = jnp.where(visible, HIGH, LOW)

    def out_copies(n, i):
        return [
            remote(
                osend.at[n, i], oin.at[y, i],
                o_send.at[dy, i], o_recv.at[dy, i], device(dy, 0, 0),
            )
            for dy in ((2,), (1, 3))[n]
        ]

    def far(i, carry):
        plane = slice(2, 4)
        keys = twice(jnp.concatenate([prompt(plane, 0), response(0)], axis=0))
        values = with_ones(jnp.concatenate([prompt(plane, PKEYS), response(SLOT)], axis=0))
        for j, s in enumerate(scores(0, i, keys)):
            s = masked(0, s)
            at = pl.ds(i * 2 * HALF + j * HALF, HALF)
            before = top[at, :]
            high = jnp.maximum(before, highest(s))
            factor = jnp.exp2(before - high)
            result = weigh(s, high[:, :1], values)
            total = acc[at, :] * jnp.concatenate([factor, factor], axis=1) + result
            finish(0, i, j, total)
        for copy in out_copies(0, i):
            copy.start()
        return carry

    lax.fori_loop(0, 2, far, 0)

    def whole(i, carry):
        for half in range(2):

            @pl.when(i == half)
            def _():
                q_copies[1, half].wait_recv()
                q_copies[3, half].wait_recv()
                load_queries(1, half)

        both = slice(0, 4)
        keys = twice(jnp.concatenate([prompt(both, 0), response(0)], axis=0))
        values = with_ones(jnp.concatenate([prompt(both, PKEYS), response(SLOT)], axis=0))
        for j, s in enumerate(scores(1, i, keys)):
            s = masked(1, s)
            finish(1, i, j, weigh(s, highest(s), values))
        for copy in out_copies(1, i):
            copy.start()
        return carry

    lax.fori_loop(0, 2, whole, 0)

    chosen = jnp.zeros((1, 1), F32)
    rejected = jnp.zeros((1, 1), F32)

    def total_of(x):
        return jnp.sum(jnp.sum(x, axis=1, keepdims=True), axis=0, keepdims=True)

    for n in range(2):
        first = qid[n] < chosen_len
        chosen = chosen + total_of(jnp.where(first, score[n], 0.0))
        rejected = rejected + total_of(jnp.where(first, 0.0, score[n]))
    lane = lax.broadcasted_iota(jnp.int32, (PAIRS, HD), 1)
    mine = lax.broadcasted_iota(jnp.int32, (PAIRS, HD), 0) == pair
    tile = jnp.where(lane == 0, chosen / chosen_len, rejected / rejected_len)
    z_place = z4 * 2 + c
    part[z_place] = jnp.where(mine & (lane < 2), tile, 0.0)
    p_copies = []
    for i, step in enumerate(column):
        copy = remote(
            part.at[z_place], part.at[z_place], p_send.at[i], p_recv.at[i], across(*step)
        )
        copy.start()
        p_copies.append(copy)
    for copy in p_copies:
        copy.wait_recv()
    sums = part[0]
    for i in range(1, 8):
        sums = sums + part[i]
    place_xy = x * NY + y
    whole_sums[place_xy] = sums
    t_copies = []
    for i, step in enumerate(plane):
        copy = remote(
            whole_sums.at[place_xy], whole_sums.at[place_xy], t_send.at[i], t_recv.at[i], across(*step)
        )
        copy.start()
        t_copies.append(copy)

    live = column_ids(y, eye) >= 0.0
    back = y >= 2
    take = jnp.where(back, SLOT - 1 - rows, rows) == cols
    place = jnp.where(live & take, 1.0, 0.0).astype(BF)

    att_copies = []

    def put(head, i, x):
        at = columns(head * 2 + i, WIDE // 2)
        k = len(att_copies)
        att[k] = dot(place, x).astype(BF)
        copy = pltpu.make_async_copy(att.at[k], att_hbm.at[:, at], att_sem.at[k])
        copy.start()
        att_copies.append(copy)

    for i in range(2):
        put(y, i, osend[0, i])
    for n, dys in enumerate(((2,), (1, 3))):
        for i in range(2):
            for copy, dy in zip(out_copies(n, i), dys):
                copy.wait_recv()
                source = (y - dy + NY) % NY
                put(source, i, oin[source, i])

    for copy in t_copies:
        copy.wait_recv()
    sums = whole_sums[0]
    for i in range(1, 16):
        sums = sums + whole_sums[i]
    value = -4.0 * (sums[:, :1] - sums[:, 1:2])
    terms = jnp.maximum(value, 0.0) + jnp.log1p(jnp.exp(-jnp.abs(value)))
    loss_ref[...] = jnp.sum(terms, axis=0, keepdims=True)

    for copy in att_copies:
        copy.wait()
    for dy in (1, 2, 3):
        kv_copies[dy].wait_send()
        r_copies[dy].wait_send()
        id_copies[dy].wait_send()
        for i in range(2):
            q_copies[dy, i].wait_send()
    for name in range(NY + 1):
        z_copies[name].wait_send()
        c_copies[name].wait_send()
        zc_copies[name].wait_send()
    for n in range(2):
        for i in range(2):
            for copy in out_copies(n, i):
                copy.wait_send()
    for copy in p_copies + t_copies:
        copy.wait_send()


def local(queries, prompt_keys, prompt_values, resp_keys, resp_values, slot_row, lengths, probe):
    vmem = pl.BlockSpec(memory_space=pltpu.VMEM)
    anywhere = pl.BlockSpec(memory_space=pl.ANY)
    sems = pltpu.SemaphoreType.DMA
    attended, loss = pl.pallas_call(
        kernel,
        out_shape=(
            jax.ShapeDtypeStruct((SLOT, QH * HD), BF),
            jax.ShapeDtypeStruct((1, 1), F32),
        ),
        in_specs=[anywhere] * 8,
        out_specs=(anywhere, vmem),
        scratch_shapes=[
            pltpu.VMEM((1, SLOT), jnp.int32),
            pltpu.VMEM((1, 2), jnp.int32),
            pltpu.VMEM((QH, HD), F32),
            pltpu.VMEM((2 * NY, SLOT, WIDE // 2), BF),
            pltpu.VMEM((4, NY, 2 * PKEYS, HD), BF),
            pltpu.VMEM((NY, RESP, HD), BF),
            pltpu.VMEM((4, 2, RESP + IDS, HD), BF),
            pltpu.VMEM((NY, IDS, SLOT), BF),
            pltpu.VMEM((NY, 2, SLOT, WIDE // 2), BF),
            pltpu.VMEM((2, WIDE, 2 * HD), BF),
            pltpu.VMEM((2, SLOT, 8 * SLOT), F32),
            pltpu.VMEM((2, SLOT, HD), F32),
            pltpu.VMEM((WIDE, HD), F32),
            pltpu.VMEM((WIDE, 2 * HD), F32),
            pltpu.VMEM((2, SLOT, HD), F32),
            pltpu.VMEM((2, 2, SLOT, WIDE // 2), BF),
            pltpu.VMEM((NY, 2, SLOT, WIDE // 2), BF),
            pltpu.VMEM((8, PAIRS, HD), F32),
            pltpu.VMEM((16, PAIRS, HD), F32),
            sems((6,)),
            sems((3,)),
            sems((2 * NY,)),
            sems((NY,)), sems((NY,)),
            sems((NY,)), sems((NY,)),
            sems((NY,)), sems((NY,)),
            sems((NY + 1,)), sems((NY + 1,)),
            sems((NY + 1,)), sems((NY + 1,)),
            sems((NY + 1,)), sems((NY + 1,)),
            sems((NY, 2)), sems((NY, 2)),
            sems((NY, 2)), sems((NY, 2)),
            sems((7,)), sems((7,)),
            sems((15,)), sems((15,)),
        ],
        compiler_params=pltpu.CompilerParams(
            collective_id=0, has_side_effects=True, vmem_limit_bytes=56 * 2**20
        ),
        cost_estimate=pl.CostEstimate(
            flops=5_400_000_000, bytes_accessed=4_000_000, transcendentals=10_500_000
        ),
    )(
        queries[0], prompt_keys[0], prompt_values[0], resp_keys[0], resp_values[0],
        slot_row, lengths, probe.reshape(QH, HD),
    )
    return attended[None], loss[0, 0]


def solution(mesh):
    return jax.shard_map(
        local,
        mesh=mesh,
        in_specs=(
            P("pair", "blk", None),
            P("pair", "blk", None),
            P("pair", "blk", None),
            P("pair", "blk", None),
            P("pair", "blk", None),
            P("pair", "blk"),
            P("pair", None),
            P(),
        ),
        out_specs=(P("pair", "blk", None), P()),
        check_vma=False,
    )
```

```python
import functools

import jax
import jax.numpy as jnp
from jax import lax
from jax.experimental import pallas as pl
from jax.experimental.pallas import tpu as pltpu
from jax.sharding import PartitionSpec as P

QH = 32
KVH = 4
HD = 128
GROUP = QH // KVH
SLOT = 128
PKEYS = 256
NY = 4
NBLK = 16
PAIRS = 8
IDS = 16
RESP = 2 * SLOT
WIDE = GROUP * HD
SCALE = 1.4426950408889634 / HD**0.5
MESH = pl.DeviceIdType.MESH
BF = jnp.bfloat16
F32 = jnp.float32
LOW = -1e30
HIGH = 3e38


def dot_t(a, b):
    return lax.dot_general(a, b, (((1,), (1,)), ((), ())), preferred_element_type=F32)


def dot(a, b):
    return jnp.dot(a, b, preferred_element_type=F32)


def kernel(
    q_hbm, kp_hbm, vp_hbm, kr_hbm, vr_hbm, slot_hbm, len_hbm, probe_hbm,
    att_hbm, loss_ref,
    slot_ref, len_ref, probe_ref, att, kv, resp, merged, ids, qin, qs, bias, qid, top, acc, score, osend, oin, part, whole_sums,
    local_sem, small_sem, att_sem, kv_send, kv_recv, r_send, r_recv, id_send, id_recv, z_send, z_recv, c_send, c_recv, zc_send, zc_recv,
    q_send, q_recv, o_send, o_recv, p_send, p_recv, t_send, t_recv,
):
    pair = lax.axis_index("pair")
    blk = lax.axis_index("blk")
    y, z, c = blk // 4, (blk // 2) % 2, blk % 2
    x, z4 = pair % 4, pair // 4 * 2 + z

    def device(dy, dz, dc):
        return (pair, ((y + dy) % NY) * 4 + ((z + dz) % 2) * 2 + (c + dc) % 2)

    def across(dx, dy, dz4, dc):
        to = (z4 + dz4) % 4
        return (
            to // 2 * 4 + (x + dx) % 4,
            ((y + dy) % NY) * 4 + (to % 2) * 2 + (c + dc) % 2,
        )

    column = [(0, 0, dz4, dc) for dz4 in range(4) for dc in range(2)][1:]
    plane = [(dx, dy, 0, 0) for dx in (2, 1, 3, 0) for dy in (2, 1, 3, 0)][:-1]

    def remote(src, dst, send, recv, target):
        return pltpu.make_async_remote_copy(
            src_ref=src, dst_ref=dst, send_sem=send, recv_sem=recv,
            device_id=target, device_id_type=MESH,
        )

    def columns(head, width):
        return pl.ds(pl.multiple_of(head * width, width), width)

    def prompt_parts(head):
        cols = columns(head, HD)
        return (
            (kp_hbm.at[:, cols], kv.at[0, y, pl.ds(0, PKEYS)]),
            (vp_hbm.at[:, cols], kv.at[0, y, pl.ds(PKEYS, PKEYS)]),
        )

    def resp_parts(head):
        cols = columns(head, HD)
        return (
            (kr_hbm.at[:, cols], resp.at[y, pl.ds(0, SLOT)]),
            (vr_hbm.at[:, cols], resp.at[y, pl.ds(SLOT, SLOT)]),
        )

    own = [
        pltpu.make_async_copy(s, d, local_sem.at[i])
        for i, (s, d) in enumerate(prompt_parts(y) + resp_parts(y))
    ]
    own_q = [
        pltpu.make_async_copy(
            q_hbm.at[:, columns(y * 2 + i, WIDE // 2)], qin.at[y, i], local_sem.at[4 + i]
        )
        for i in range(2)
    ]
    for copy in own + own_q:
        copy.start()
    small = [
        pltpu.make_async_copy(s, d, small_sem.at[i])
        for i, (s, d) in enumerate(
            ((slot_hbm, slot_ref), (len_hbm, len_ref), (probe_hbm, probe_ref))
        )
    ]
    for copy in small:
        copy.start()

    barrier = pltpu.get_barrier_semaphore()
    for step in column + plane:
        pl.semaphore_signal(barrier, inc=1, device_id=across(*step), device_id_type=MESH)
    small[0].wait()
    shifted = jnp.broadcast_to(slot_ref[...] + 32, (IDS, SLOT))
    upper = lax.broadcasted_iota(jnp.int32, (IDS, SLOT), 0) < IDS // 2
    ids[y] = jnp.where(upper, shifted >> 5, shifted & 31).astype(F32).astype(BF)
    pl.semaphore_wait(barrier, len(column) + len(plane))

    kv_copies, r_copies, q_copies = {}, {}, {}

    def send_prompt(dy):
        to = device(dy, 0, 0)
        for s, d in prompt_parts((y + dy) % NY):
            remote(s, d, kv_send.at[dy], kv_recv.at[dy], to).start()
        kv_copies[dy] = remote(kv.at[0, y], kv.at[0, y], kv_send.at[dy], kv_recv.at[dy], to)

    def send_resp(dy):
        to = device(dy, 0, 0)
        for s, d in resp_parts((y + dy) % NY):
            remote(s, d, r_send.at[dy], r_recv.at[dy], to).start()
        r_copies[dy] = remote(resp.at[y], resp.at[y], r_send.at[dy], r_recv.at[dy], to)

    for dy in (1, 2, 3):
        for i in range(2):
            q_copies[dy, i] = remote(
                q_hbm.at[:, columns(((y + dy) % NY) * 2 + i, WIDE // 2)], qin.at[y, i],
                q_send.at[dy, i], q_recv.at[dy, i], device(dy, 0, 0),
            )

    def send_queries(dy, i):
        q_copies[dy, i].start()

    id_copies = {
        dy: remote(ids.at[y], ids.at[y], id_send.at[dy], id_recv.at[dy], device(dy, 0, 0))
        for dy in (1, 2, 3)
    }
    send_prompt(1)
    send_prompt(3)
    for dy in (1, 2, 3):
        id_copies[dy].start()

    z_copies, c_copies, zc_copies = {}, {}, {}

    def pass_on(name, piece):
        z_copies[name] = remote(
            piece(0), piece(2), z_send.at[name], z_recv.at[name], device(0, 1, 0)
        )
        c_copies[name] = remote(
            piece(0), piece(1), c_send.at[name], c_recv.at[name], device(0, 0, 1)
        )
        zc_copies[name] = remote(
            piece(2), piece(3), zc_send.at[name], zc_recv.at[name], device(0, 0, 1)
        )

    def start_on(name):
        z_copies[name].start()
        c_copies[name].start()

    def forward(dy):
        at = (y - dy + NY) % NY
        pass_on(dy, lambda group: kv.at[group, at])
        start_on(dy)

    for copy in own:
        copy.wait()
    forward(0)

    c_copies[0].wait_recv()
    send_prompt(2)
    for dy in (1, 3):
        kv_copies[dy].wait_recv()
        forward(dy)
    for dy in (2, 1, 3):
        send_resp(dy)
    kv_copies[2].wait_recv()
    forward(2)
    c_copies[2].wait_recv()
    send_queries(2, 0)

    rows = lax.broadcasted_iota(jnp.int32, (SLOT, SLOT), 0)
    cols = lax.broadcasted_iota(jnp.int32, (SLOT, SLOT), 1)
    eye = jnp.where(rows == cols, 1.0, 0.0).astype(BF)
    turn = jnp.where(rows + cols == SLOT - 1, 1.0, 0.0).astype(BF)
    half_ids = IDS // 2

    def column_ids(slot, order):
        t = dot_t(order, ids[slot])
        return 32.0 * t[:, :1] + t[:, half_ids : half_ids + 1] - 32.0

    def row_ids(t):
        return 32.0 * t[:1] + t[half_ids : half_ids + 1] - 32.0

    pass_on(NY, lambda group: merged.at[group])

    for dy in (1, 2, 3):
        id_copies[dy].wait_recv()
    for dy in (1, 3, 2):
        r_copies[dy].wait_recv()
    for j in range(2):
        live = column_ids(j, eye) >= 0.0
        for part_of in range(2):
            at = slice(part_of * SLOT, (part_of + 1) * SLOT)
            one = resp[j, at, :].astype(F32)
            two = dot(turn, resp[j + 2, at, :])
            merged[0, j, at, :] = jnp.where(live, one, two).astype(BF)
        one = ids[j].astype(F32)
        two = dot(ids[j + 2], turn)
        merged[0, j, RESP:, :] = jnp.where(row_ids(one) >= 0.0, one, two).astype(BF)
    start_on(NY)
    send_queries(2, 1)

    firsts = (y % 2, (y + 1) % 2)

    def load_queries(n, i):
        first = firsts[n]
        live = column_ids(first, eye) >= 0.0
        back = dot(turn, qin[first + 2, i])
        for h in range(GROUP // 2):
            at = slice(h * HD, (h + 1) * HD)
            to = slice((i * (GROUP // 2) + h) * HD, (i * (GROUP // 2) + h + 1) * HD)
            x = jnp.where(live, qin[first, i, :, at].astype(F32), back[:, at]) * SCALE
            high = x.astype(BF)
            qs[n, to, :HD] = high
            qs[n, to, HD:] = (x - high.astype(F32)).astype(BF)

    def twice(k):
        return jnp.concatenate([k, k], axis=1)

    def with_ones(v):
        return jnp.concatenate([v, jnp.ones_like(v)], axis=1)

    def prompt(groups, at):
        part = kv[groups, :, at : at + PKEYS, :]
        return part.reshape(part.shape[0] * NY * PKEYS, HD)

    def response(at):
        return merged[:, :, at : at + SLOT, :].reshape(8 * SLOT, HD)

    HALF = 2 * HD

    def scores(n, i, keys):
        q = [qs[n, pl.ds(i * 2 * HALF + j * HALF, HALF), :] for j in range(2)]
        return [dot_t(x, keys) for x in q]

    def masked(n, s):
        at = s.shape[1] - 8 * SLOT
        limit = bias[n]
        limit = jnp.concatenate([limit, limit], axis=0)
        return jnp.concatenate([s[:, :at], jnp.minimum(s[:, at:], limit)], axis=1)

    def highest(s):
        return jnp.max(s, axis=1, keepdims=True)

    def weigh(s, high, values):
        return dot(jnp.exp2(s - high).astype(BF), values)

    def finish(n, i, j, result):
        out = (result[:, :HD] / result[:, HD:]).astype(BF)
        for h in range(2):
            head = 2 * j + h
            x = out[h * HD : (h + 1) * HD]
            osend[n, i, :, head * HD : (head + 1) * HD] = x
            weights = probe_ref[pl.ds(y * GROUP + i * 4 + head, 1), :]
            score[n] = score[n] + x.astype(F32) * weights

    score[...] = jnp.zeros_like(score)

    def take_z(name):
        z_copies[name].wait_recv()
        zc_copies[name].start()

    def near(k, carry):
        @pl.when(k == 0)
        def _():
            own_q[0].wait()
            q_copies[2, 0].wait_recv()
            send_queries(1, 0)
            send_queries(3, 0)
            load_queries(0, 0)
            for dy in (1, 3):
                c_copies[dy].wait_recv()

        @pl.when(k == 1)
        def _():
            for name in (0, 1, 3, 2, NY):
                take_z(name)
            own_q[1].wait()
            q_copies[2, 1].wait_recv()
            send_queries(1, 1)
            send_queries(3, 1)
            load_queries(0, 1)

        plane = slice(0, 2)
        keys, values = twice(prompt(plane, 0)), with_ones(prompt(plane, PKEYS))
        for j, s in enumerate(scores(0, k, keys)):
            high = highest(s)
            at = pl.ds(k * 2 * HALF + j * HALF, HALF)
            top[at, :] = jnp.broadcast_to(high, (HALF, HD))
            acc[at, :] = weigh(s, high, values)
        return carry

    lax.fori_loop(0, 2, near, 0)

    c_copies[NY].wait_recv()
    for name in range(NY + 1):
        zc_copies[name].wait_recv()

    id_rows = [
        row_ids(merged[g, j, RESP:, :].astype(F32)) for g in range(4) for j in range(2)
    ]
    small[1].wait()
    small[2].wait()
    chosen_len = len_ref[:1, :1].astype(F32)
    rejected_len = len_ref[:1, 1:2].astype(F32)
    for n in range(2):
        t = dot_t(eye, merged[0, firsts[n], RESP:, :])
        row_of = 32.0 * t[:, :1] + t[:, half_ids : half_ids + 1] - 32.0
        lowest = jnp.where(row_of >= chosen_len, chosen_len, 0.0)
        qid[n] = jnp.broadcast_to(row_of, (SLOT, HD))
        for m in range(8):
            visible = (id_rows[m] <= row_of) & (id_rows[m] >= lowest)
            bias[n, :, m * SLOT : (m + 1) * SLOT] = jnp.where(visible, HIGH, LOW)

    def out_copies(n, i):
        return [
            remote(
                osend.at[n, i], oin.at[y, i],
                o_send.at[dy, i], o_recv.at[dy, i], device(dy, 0, 0),
            )
            for dy in ((2,), (1, 3))[n]
        ]

    plane_keys = slice(2, 4)
    keys = twice(jnp.concatenate([prompt(plane_keys, 0), response(0)], axis=0))
    values = with_ones(jnp.concatenate([prompt(plane_keys, PKEYS), response(SLOT)], axis=0))
    first = scores(0, 0, keys)
    second = scores(0, 1, keys)
    for i, ss in enumerate((first, second)):
        for j, s in enumerate(ss):
            s = masked(0, s)
            at = pl.ds(i * 2 * HALF + j * HALF, HALF)
            before = top[at, :]
            high = jnp.maximum(before, highest(s))
            factor = jnp.exp2(before - high)
            result = weigh(s, high[:, :1], values)
            total = acc[at, :] * jnp.concatenate([factor, factor], axis=1) + result
            finish(0, i, j, total)
        for copy in out_copies(0, i):
            copy.start()

    for half in range(2):
        q_copies[1, half].wait_recv()
        q_copies[3, half].wait_recv()
        load_queries(1, half)
    both = slice(0, 4)
    keys = twice(jnp.concatenate([prompt(both, 0), response(0)], axis=0))
    values = with_ones(jnp.concatenate([prompt(both, PKEYS), response(SLOT)], axis=0))
    first = scores(1, 0, keys)
    second = scores(1, 1, keys)
    for i, ss in enumerate((first, second)):
        for j, s in enumerate(ss):
            s = masked(1, s)
            finish(1, i, j, weigh(s, highest(s), values))
        for copy in out_copies(1, i):
            copy.start()

    chosen = jnp.zeros((1, 1), F32)
    rejected = jnp.zeros((1, 1), F32)

    def total_of(x):
        return jnp.sum(jnp.sum(x, axis=1, keepdims=True), axis=0, keepdims=True)

    for n in range(2):
        first = qid[n] < chosen_len
        chosen = chosen + total_of(jnp.where(first, score[n], 0.0))
        rejected = rejected + total_of(jnp.where(first, 0.0, score[n]))
    lane = lax.broadcasted_iota(jnp.int32, (PAIRS, HD), 1)
    mine = lax.broadcasted_iota(jnp.int32, (PAIRS, HD), 0) == pair
    tile = jnp.where(lane == 0, chosen / chosen_len, rejected / rejected_len)
    z_place = z4 * 2 + c
    part[z_place] = jnp.where(mine & (lane < 2), tile, 0.0)
    p_copies = []
    for i, step in enumerate(column):
        copy = remote(
            part.at[z_place], part.at[z_place], p_send.at[i], p_recv.at[i], across(*step)
        )
        copy.start()
        p_copies.append(copy)
    for copy in p_copies:
        copy.wait_recv()
    sums = part[0]
    for i in range(1, 8):
        sums = sums + part[i]
    place_xy = x * NY + y
    whole_sums[place_xy] = sums
    t_copies = []
    for i, step in enumerate(plane):
        copy = remote(
            whole_sums.at[place_xy], whole_sums.at[place_xy], t_send.at[i], t_recv.at[i], across(*step)
        )
        copy.start()
        t_copies.append(copy)

    live = column_ids(y, eye) >= 0.0
    back = y >= 2
    take = jnp.where(back, SLOT - 1 - rows, rows) == cols
    place = jnp.where(live & take, 1.0, 0.0).astype(BF)

    att_copies = []

    def put(head, i, x):
        at = columns(head * 2 + i, WIDE // 2)
        k = len(att_copies)
        att[k] = dot(place, x).astype(BF)
        copy = pltpu.make_async_copy(att.at[k], att_hbm.at[:, at], att_sem.at[k])
        copy.start()
        att_copies.append(copy)

    for i in range(2):
        put(y, i, osend[0, i])
    for n, dys in enumerate(((2,), (1, 3))):
        for i in range(2):
            for copy, dy in zip(out_copies(n, i), dys):
                copy.wait_recv()
                source = (y - dy + NY) % NY
                put(source, i, oin[source, i])

    for copy in t_copies:
        copy.wait_recv()
    sums = whole_sums[0]
    for i in range(1, 16):
        sums = sums + whole_sums[i]
    value = -4.0 * (sums[:, :1] - sums[:, 1:2])
    terms = jnp.maximum(value, 0.0) + jnp.log1p(jnp.exp(-jnp.abs(value)))
    loss_ref[...] = jnp.sum(terms, axis=0, keepdims=True)

    for copy in att_copies:
        copy.wait()
    for dy in (1, 2, 3):
        kv_copies[dy].wait_send()
        r_copies[dy].wait_send()
        id_copies[dy].wait_send()
        for i in range(2):
            q_copies[dy, i].wait_send()
    for name in range(NY + 1):
        z_copies[name].wait_send()
        c_copies[name].wait_send()
        zc_copies[name].wait_send()
    for n in range(2):
        for i in range(2):
            for copy in out_copies(n, i):
                copy.wait_send()
    for copy in p_copies + t_copies:
        copy.wait_send()


def local(queries, prompt_keys, prompt_values, resp_keys, resp_values, slot_row, lengths, probe):
    vmem = pl.BlockSpec(memory_space=pltpu.VMEM)
    anywhere = pl.BlockSpec(memory_space=pl.ANY)
    sems = pltpu.SemaphoreType.DMA
    attended, loss = pl.pallas_call(
        kernel,
        out_shape=(
            jax.ShapeDtypeStruct((SLOT, QH * HD), BF),
            jax.ShapeDtypeStruct((1, 1), F32),
        ),
        in_specs=[anywhere] * 8,
        out_specs=(anywhere, vmem),
        scratch_shapes=[
            pltpu.VMEM((1, SLOT), jnp.int32),
            pltpu.VMEM((1, 2), jnp.int32),
            pltpu.VMEM((QH, HD), F32),
            pltpu.VMEM((2 * NY, SLOT, WIDE // 2), BF),
            pltpu.VMEM((4, NY, 2 * PKEYS, HD), BF),
            pltpu.VMEM((NY, RESP, HD), BF),
            pltpu.VMEM((4, 2, RESP + IDS, HD), BF),
            pltpu.VMEM((NY, IDS, SLOT), BF),
            pltpu.VMEM((NY, 2, SLOT, WIDE // 2), BF),
            pltpu.VMEM((2, WIDE, 2 * HD), BF),
            pltpu.VMEM((2, SLOT, 8 * SLOT), F32),
            pltpu.VMEM((2, SLOT, HD), F32),
            pltpu.VMEM((WIDE, HD), F32),
            pltpu.VMEM((WIDE, 2 * HD), F32),
            pltpu.VMEM((2, SLOT, HD), F32),
            pltpu.VMEM((2, 2, SLOT, WIDE // 2), BF),
            pltpu.VMEM((NY, 2, SLOT, WIDE // 2), BF),
            pltpu.VMEM((8, PAIRS, HD), F32),
            pltpu.VMEM((16, PAIRS, HD), F32),
            sems((6,)),
            sems((3,)),
            sems((2 * NY,)),
            sems((NY,)), sems((NY,)),
            sems((NY,)), sems((NY,)),
            sems((NY,)), sems((NY,)),
            sems((NY + 1,)), sems((NY + 1,)),
            sems((NY + 1,)), sems((NY + 1,)),
            sems((NY + 1,)), sems((NY + 1,)),
            sems((NY, 2)), sems((NY, 2)),
            sems((NY, 2)), sems((NY, 2)),
            sems((7,)), sems((7,)),
            sems((15,)), sems((15,)),
        ],
        compiler_params=pltpu.CompilerParams(
            collective_id=0, has_side_effects=True, vmem_limit_bytes=56 * 2**20
        ),
        cost_estimate=pl.CostEstimate(
            flops=5_400_000_000, bytes_accessed=4_000_000, transcendentals=10_500_000
        ),
    )(
        queries[0], prompt_keys[0], prompt_values[0], resp_keys[0], resp_values[0],
        slot_row, lengths, probe.reshape(QH, HD),
    )
    return attended[None], loss[0, 0]


def solution(mesh):
    return jax.shard_map(
        local,
        mesh=mesh,
        in_specs=(
            P("pair", "blk", None),
            P("pair", "blk", None),
            P("pair", "blk", None),
            P("pair", "blk", None),
            P("pair", "blk", None),
            P("pair", "blk"),
            P("pair", None),
            P(),
        ),
        out_specs=(P("pair", "blk", None), P()),
        check_vma=False,
    )
```

```python
import functools

import jax
import jax.numpy as jnp
from jax import lax
from jax.experimental import pallas as pl
from jax.experimental.pallas import tpu as pltpu
from jax.sharding import PartitionSpec as P

QH = 32
KVH = 4
HD = 128
GROUP = QH // KVH
SLOT = 128
PKEYS = 256
NY = 4
NBLK = 16
PAIRS = 8
IDS = 16
RESP = 2 * SLOT
WIDE = GROUP * HD
SCALE = 1.4426950408889634 / HD**0.5
MESH = pl.DeviceIdType.MESH
BF = jnp.bfloat16
F32 = jnp.float32
LOW = -1e30
HIGH = 3e38


def dot_t(a, b):
    return lax.dot_general(a, b, (((1,), (1,)), ((), ())), preferred_element_type=F32)


def dot(a, b):
    return jnp.dot(a, b, preferred_element_type=F32)


def kernel(
    q_hbm, kp_hbm, vp_hbm, kr_hbm, vr_hbm, slot_hbm, len_hbm, probe_hbm,
    att_hbm, loss_ref,
    slot_ref, len_ref, probe_ref, att, kv, resp, merged, ids, qin, qs, bias, qid, top, acc, score, osend, oin, part, whole_sums,
    local_sem, small_sem, att_sem, kv_send, kv_recv, r_send, r_recv, id_send, id_recv, z_send, z_recv, c_send, c_recv, zc_send, zc_recv,
    q_send, q_recv, o_send, o_recv, p_send, p_recv, t_send, t_recv,
):
    pair = lax.axis_index("pair")
    blk = lax.axis_index("blk")
    y, z, c = blk // 4, (blk // 2) % 2, blk % 2
    x, z4 = pair % 4, pair // 4 * 2 + z

    def device(dy, dz, dc):
        return (pair, ((y + dy) % NY) * 4 + ((z + dz) % 2) * 2 + (c + dc) % 2)

    def across(dx, dy, dz4, dc):
        to = (z4 + dz4) % 4
        return (
            to // 2 * 4 + (x + dx) % 4,
            ((y + dy) % NY) * 4 + (to % 2) * 2 + (c + dc) % 2,
        )

    column = [(0, 0, dz4, dc) for dz4 in range(4) for dc in range(2)][1:]
    plane = [(dx, dy, 0, 0) for dx in (2, 1, 3, 0) for dy in (2, 1, 3, 0)][:-1]

    def remote(src, dst, send, recv, target):
        return pltpu.make_async_remote_copy(
            src_ref=src, dst_ref=dst, send_sem=send, recv_sem=recv,
            device_id=target, device_id_type=MESH,
        )

    def columns(head, width):
        return pl.ds(pl.multiple_of(head * width, width), width)

    def prompt_parts(head):
        cols = columns(head, HD)
        return (
            (kp_hbm.at[:, cols], kv.at[0, y, pl.ds(0, PKEYS)]),
            (vp_hbm.at[:, cols], kv.at[0, y, pl.ds(PKEYS, PKEYS)]),
        )

    def resp_parts(head):
        cols = columns(head, HD)
        return (
            (kr_hbm.at[:, cols], resp.at[y, pl.ds(0, SLOT)]),
            (vr_hbm.at[:, cols], resp.at[y, pl.ds(SLOT, SLOT)]),
        )

    own = [
        pltpu.make_async_copy(s, d, local_sem.at[i])
        for i, (s, d) in enumerate(prompt_parts(y) + resp_parts(y))
    ]
    own_q = [
        pltpu.make_async_copy(
            q_hbm.at[:, columns(y * 2 + i, WIDE // 2)], qin.at[y, i], local_sem.at[4 + i]
        )
        for i in range(2)
    ]
    for copy in own + own_q:
        copy.start()
    small = [
        pltpu.make_async_copy(s, d, small_sem.at[i])
        for i, (s, d) in enumerate(
            ((slot_hbm, slot_ref), (len_hbm, len_ref), (probe_hbm, probe_ref))
        )
    ]
    for copy in small:
        copy.start()

    barrier = pltpu.get_barrier_semaphore()
    for step in column + plane:
        pl.semaphore_signal(barrier, inc=1, device_id=across(*step), device_id_type=MESH)
    small[0].wait()
    shifted = jnp.broadcast_to(slot_ref[...] + 32, (IDS, SLOT))
    upper = lax.broadcasted_iota(jnp.int32, (IDS, SLOT), 0) < IDS // 2
    ids[y] = jnp.where(upper, shifted >> 5, shifted & 31).astype(F32).astype(BF)
    pl.semaphore_wait(barrier, len(column) + len(plane))

    kv_copies, r_copies, q_copies = {}, {}, {}

    def send_prompt(dy):
        to = device(dy, 0, 0)
        for s, d in prompt_parts((y + dy) % NY):
            remote(s, d, kv_send.at[dy], kv_recv.at[dy], to).start()
        kv_copies[dy] = remote(kv.at[0, y], kv.at[0, y], kv_send.at[dy], kv_recv.at[dy], to)

    def send_resp(dy):
        to = device(dy, 0, 0)
        for s, d in resp_parts((y + dy) % NY):
            remote(s, d, r_send.at[dy], r_recv.at[dy], to).start()
        r_copies[dy] = remote(resp.at[y], resp.at[y], r_send.at[dy], r_recv.at[dy], to)

    for dy in (1, 2, 3):
        for i in range(2):
            q_copies[dy, i] = remote(
                q_hbm.at[:, columns(((y + dy) % NY) * 2 + i, WIDE // 2)], qin.at[y, i],
                q_send.at[dy, i], q_recv.at[dy, i], device(dy, 0, 0),
            )

    def send_queries(dy, i):
        q_copies[dy, i].start()

    id_copies = {
        dy: remote(ids.at[y], ids.at[y], id_send.at[dy], id_recv.at[dy], device(dy, 0, 0))
        for dy in (1, 2, 3)
    }
    send_prompt(1)
    send_prompt(3)
    for dy in (1, 2, 3):
        id_copies[dy].start()

    z_copies, c_copies, zc_copies = {}, {}, {}

    def pass_on(name, piece):
        z_copies[name] = remote(
            piece(0), piece(2), z_send.at[name], z_recv.at[name], device(0, 1, 0)
        )
        c_copies[name] = remote(
            piece(0), piece(1), c_send.at[name], c_recv.at[name], device(0, 0, 1)
        )
        zc_copies[name] = remote(
            piece(2), piece(3), zc_send.at[name], zc_recv.at[name], device(0, 0, 1)
        )

    def start_on(name):
        z_copies[name].start()
        c_copies[name].start()

    def forward(dy):
        at = (y - dy + NY) % NY
        pass_on(dy, lambda group: kv.at[group, at])
        start_on(dy)

    for copy in own:
        copy.wait()
    forward(0)

    c_copies[0].wait_recv()
    send_prompt(2)
    for dy in (1, 3):
        kv_copies[dy].wait_recv()
        forward(dy)
    for dy in (2, 1, 3):
        send_resp(dy)
    kv_copies[2].wait_recv()
    forward(2)
    c_copies[2].wait_recv()
    send_queries(2, 0)

    rows = lax.broadcasted_iota(jnp.int32, (SLOT, SLOT), 0)
    cols = lax.broadcasted_iota(jnp.int32, (SLOT, SLOT), 1)
    eye = jnp.where(rows == cols, 1.0, 0.0).astype(BF)
    turn = jnp.where(rows + cols == SLOT - 1, 1.0, 0.0).astype(BF)
    half_ids = IDS // 2

    def column_ids(slot, order):
        t = dot_t(order, ids[slot])
        return 32.0 * t[:, :1] + t[:, half_ids : half_ids + 1] - 32.0

    def row_ids(t):
        return 32.0 * t[:1] + t[half_ids : half_ids + 1] - 32.0

    pass_on(NY, lambda group: merged.at[group])

    for dy in (1, 2, 3):
        id_copies[dy].wait_recv()
    for dy in (1, 3, 2):
        r_copies[dy].wait_recv()
    for j in range(2):
        live = column_ids(j, eye) >= 0.0
        for part_of in range(2):
            at = slice(part_of * SLOT, (part_of + 1) * SLOT)
            one = resp[j, at, :].astype(F32)
            two = dot(turn, resp[j + 2, at, :])
            merged[0, j, at, :] = jnp.where(live, one, two).astype(BF)
        one = ids[j].astype(F32)
        two = dot(ids[j + 2], turn)
        merged[0, j, RESP:, :] = jnp.where(row_ids(one) >= 0.0, one, two).astype(BF)
    start_on(NY)
    send_queries(2, 1)

    firsts = (y % 2, (y + 1) % 2)

    def load_queries(n, i):
        first = firsts[n]
        live = column_ids(first, eye) >= 0.0
        back = dot(turn, qin[first + 2, i])
        for h in range(GROUP // 2):
            at = slice(h * HD, (h + 1) * HD)
            to = slice((i * (GROUP // 2) + h) * HD, (i * (GROUP // 2) + h + 1) * HD)
            x = jnp.where(live, qin[first, i, :, at].astype(F32), back[:, at]) * SCALE
            high = x.astype(BF)
            qs[n, to, :HD] = high
            qs[n, to, HD:] = (x - high.astype(F32)).astype(BF)

    def twice(k):
        return jnp.concatenate([k, k], axis=1)

    def with_ones(v):
        return jnp.concatenate([v, jnp.ones_like(v)], axis=1)

    def prompt(groups, at):
        part = kv[groups, :, at : at + PKEYS, :]
        return part.reshape(part.shape[0] * NY * PKEYS, HD)

    def response(at):
        return merged[:, :, at : at + SLOT, :].reshape(8 * SLOT, HD)

    HALF = 2 * HD

    def scores(n, i, keys):
        q = [qs[n, pl.ds(i * 2 * HALF + j * HALF, HALF), :] for j in range(2)]
        return [dot_t(x, keys) for x in q]

    def masked(n, s):
        at = s.shape[1] - 8 * SLOT
        limit = bias[n]
        limit = jnp.concatenate([limit, limit], axis=0)
        return jnp.concatenate([s[:, :at], jnp.minimum(s[:, at:], limit)], axis=1)

    def highest(s):
        return jnp.max(s, axis=1, keepdims=True)

    def weigh(s, high, values):
        return dot(jnp.exp2(s - high).astype(BF), values)

    def finish(n, i, j, result):
        out = (result[:, :HD] / result[:, HD:]).astype(BF)
        for h in range(2):
            head = 2 * j + h
            x = out[h * HD : (h + 1) * HD]
            osend[n, i, :, head * HD : (head + 1) * HD] = x
            weights = probe_ref[pl.ds(y * GROUP + i * 4 + head, 1), :]
            score[n] = score[n] + x.astype(F32) * weights

    score[...] = jnp.zeros_like(score)

    def take_z(name):
        z_copies[name].wait_recv()
        zc_copies[name].start()

    def near(k, carry):
        @pl.when(k == 0)
        def _():
            own_q[0].wait()
            q_copies[2, 0].wait_recv()
            send_queries(1, 0)
            send_queries(3, 0)
            load_queries(0, 0)
            for dy in (1, 3):
                c_copies[dy].wait_recv()

        @pl.when(k == 1)
        def _():
            for name in (0, 1, 3, 2, NY):
                take_z(name)
            own_q[1].wait()
            q_copies[2, 1].wait_recv()
            send_queries(1, 1)
            send_queries(3, 1)
            load_queries(0, 1)

        plane = slice(0, 2)
        keys, values = twice(prompt(plane, 0)), with_ones(prompt(plane, PKEYS))
        for j, s in enumerate(scores(0, k, keys)):
            high = highest(s)
            at = pl.ds(k * 2 * HALF + j * HALF, HALF)
            top[at, :] = jnp.broadcast_to(high, (HALF, HD))
            acc[at, :] = weigh(s, high, values)
        return carry

    lax.fori_loop(0, 2, near, 0)

    c_copies[NY].wait_recv()
    small[1].wait()
    small[2].wait()
    chosen_len = len_ref[:1, :1].astype(F32)
    rejected_len = len_ref[:1, 1:2].astype(F32)
    seen = []
    for n in range(2):
        t = dot_t(eye, merged[0, firsts[n], RESP:, :])
        row_of = 32.0 * t[:, :1] + t[:, half_ids : half_ids + 1] - 32.0
        qid[n] = jnp.broadcast_to(row_of, (SLOT, HD))
        seen.append((row_of, jnp.where(row_of >= chosen_len, chosen_len, 0.0)))

    def mask(group):
        for j in range(2):
            row = row_ids(merged[group, j, RESP:, :].astype(F32))
            at = slice((2 * group + j) * SLOT, (2 * group + j + 1) * SLOT)
            for n, (row_of, lowest) in enumerate(seen):
                visible = (row <= row_of) & (row >= lowest)
                bias[n, :, at] = jnp.where(visible, HIGH, LOW)

    for group in range(3):
        mask(group)
    for name in range(NY + 1):
        zc_copies[name].wait_recv()
    mask(3)

    def out_copies(n, i):
        return [
            remote(
                osend.at[n, i], oin.at[y, i],
                o_send.at[dy, i], o_recv.at[dy, i], device(dy, 0, 0),
            )
            for dy in ((2,), (1, 3))[n]
        ]

    plane_keys = slice(2, 4)
    keys = twice(jnp.concatenate([prompt(plane_keys, 0), response(0)], axis=0))
    values = with_ones(jnp.concatenate([prompt(plane_keys, PKEYS), response(SLOT)], axis=0))
    first = scores(0, 0, keys)
    second = scores(0, 1, keys)
    for i, ss in enumerate((first, second)):
        for j, s in enumerate(ss):
            s = masked(0, s)
            at = pl.ds(i * 2 * HALF + j * HALF, HALF)
            before = top[at, :]
            high = jnp.maximum(before, highest(s))
            factor = jnp.exp2(before - high)
            result = weigh(s, high[:, :1], values)
            total = acc[at, :] * jnp.concatenate([factor, factor], axis=1) + result
            finish(0, i, j, total)
        for copy in out_copies(0, i):
            copy.start()

    for half in range(2):
        q_copies[1, half].wait_recv()
        q_copies[3, half].wait_recv()
        load_queries(1, half)
    both = slice(0, 4)
    keys = twice(jnp.concatenate([prompt(both, 0), response(0)], axis=0))
    values = with_ones(jnp.concatenate([prompt(both, PKEYS), response(SLOT)], axis=0))
    first = scores(1, 0, keys)
    second = scores(1, 1, keys)
    for i, ss in enumerate((first, second)):
        for j, s in enumerate(ss):
            s = masked(1, s)
            finish(1, i, j, weigh(s, highest(s), values))
        for copy in out_copies(1, i):
            copy.start()

    chosen = jnp.zeros((1, 1), F32)
    rejected = jnp.zeros((1, 1), F32)

    def total_of(x):
        return jnp.sum(jnp.sum(x, axis=1, keepdims=True), axis=0, keepdims=True)

    for n in range(2):
        first = qid[n] < chosen_len
        chosen = chosen + total_of(jnp.where(first, score[n], 0.0))
        rejected = rejected + total_of(jnp.where(first, 0.0, score[n]))
    lane = lax.broadcasted_iota(jnp.int32, (PAIRS, HD), 1)
    mine = lax.broadcasted_iota(jnp.int32, (PAIRS, HD), 0) == pair
    tile = jnp.where(lane == 0, chosen / chosen_len, rejected / rejected_len)
    z_place = z4 * 2 + c
    part[z_place] = jnp.where(mine & (lane < 2), tile, 0.0)
    p_copies = []
    for i, step in enumerate(column):
        copy = remote(
            part.at[z_place], part.at[z_place], p_send.at[i], p_recv.at[i], across(*step)
        )
        copy.start()
        p_copies.append(copy)
    for copy in p_copies:
        copy.wait_recv()
    sums = part[0]
    for i in range(1, 8):
        sums = sums + part[i]
    place_xy = x * NY + y
    whole_sums[place_xy] = sums
    t_copies = []
    for i, step in enumerate(plane):
        copy = remote(
            whole_sums.at[place_xy], whole_sums.at[place_xy], t_send.at[i], t_recv.at[i], across(*step)
        )
        copy.start()
        t_copies.append(copy)

    live = column_ids(y, eye) >= 0.0
    back = y >= 2
    take = jnp.where(back, SLOT - 1 - rows, rows) == cols
    place = jnp.where(live & take, 1.0, 0.0).astype(BF)

    att_copies = []

    def put(head, i, x):
        at = columns(head * 2 + i, WIDE // 2)
        k = len(att_copies)
        att[k] = dot(place, x).astype(BF)
        copy = pltpu.make_async_copy(att.at[k], att_hbm.at[:, at], att_sem.at[k])
        copy.start()
        att_copies.append(copy)

    for i in range(2):
        put(y, i, osend[0, i])
    for n, dys in enumerate(((2,), (1, 3))):
        for i in range(2):
            for copy, dy in zip(out_copies(n, i), dys):
                copy.wait_recv()
                source = (y - dy + NY) % NY
                put(source, i, oin[source, i])

    for copy in t_copies:
        copy.wait_recv()
    sums = whole_sums[0]
    for i in range(1, 16):
        sums = sums + whole_sums[i]
    value = -4.0 * (sums[:, :1] - sums[:, 1:2])
    terms = jnp.maximum(value, 0.0) + jnp.log1p(jnp.exp(-jnp.abs(value)))
    loss_ref[...] = jnp.sum(terms, axis=0, keepdims=True)

    for copy in att_copies:
        copy.wait()
    for dy in (1, 2, 3):
        kv_copies[dy].wait_send()
        r_copies[dy].wait_send()
        id_copies[dy].wait_send()
        for i in range(2):
            q_copies[dy, i].wait_send()
    for name in range(NY + 1):
        z_copies[name].wait_send()
        c_copies[name].wait_send()
        zc_copies[name].wait_send()
    for n in range(2):
        for i in range(2):
            for copy in out_copies(n, i):
                copy.wait_send()
    for copy in p_copies + t_copies:
        copy.wait_send()


def local(queries, prompt_keys, prompt_values, resp_keys, resp_values, slot_row, lengths, probe):
    vmem = pl.BlockSpec(memory_space=pltpu.VMEM)
    anywhere = pl.BlockSpec(memory_space=pl.ANY)
    sems = pltpu.SemaphoreType.DMA
    attended, loss = pl.pallas_call(
        kernel,
        out_shape=(
            jax.ShapeDtypeStruct((SLOT, QH * HD), BF),
            jax.ShapeDtypeStruct((1, 1), F32),
        ),
        in_specs=[anywhere] * 8,
        out_specs=(anywhere, vmem),
        scratch_shapes=[
            pltpu.VMEM((1, SLOT), jnp.int32),
            pltpu.VMEM((1, 2), jnp.int32),
            pltpu.VMEM((QH, HD), F32),
            pltpu.VMEM((2 * NY, SLOT, WIDE // 2), BF),
            pltpu.VMEM((4, NY, 2 * PKEYS, HD), BF),
            pltpu.VMEM((NY, RESP, HD), BF),
            pltpu.VMEM((4, 2, RESP + IDS, HD), BF),
            pltpu.VMEM((NY, IDS, SLOT), BF),
            pltpu.VMEM((NY, 2, SLOT, WIDE // 2), BF),
            pltpu.VMEM((2, WIDE, 2 * HD), BF),
            pltpu.VMEM((2, SLOT, 8 * SLOT), F32),
            pltpu.VMEM((2, SLOT, HD), F32),
            pltpu.VMEM((WIDE, HD), F32),
            pltpu.VMEM((WIDE, 2 * HD), F32),
            pltpu.VMEM((2, SLOT, HD), F32),
            pltpu.VMEM((2, 2, SLOT, WIDE // 2), BF),
            pltpu.VMEM((NY, 2, SLOT, WIDE // 2), BF),
            pltpu.VMEM((8, PAIRS, HD), F32),
            pltpu.VMEM((16, PAIRS, HD), F32),
            sems((6,)),
            sems((3,)),
            sems((2 * NY,)),
            sems((NY,)), sems((NY,)),
            sems((NY,)), sems((NY,)),
            sems((NY,)), sems((NY,)),
            sems((NY + 1,)), sems((NY + 1,)),
            sems((NY + 1,)), sems((NY + 1,)),
            sems((NY + 1,)), sems((NY + 1,)),
            sems((NY, 2)), sems((NY, 2)),
            sems((NY, 2)), sems((NY, 2)),
            sems((7,)), sems((7,)),
            sems((15,)), sems((15,)),
        ],
        compiler_params=pltpu.CompilerParams(
            collective_id=0, has_side_effects=True, vmem_limit_bytes=56 * 2**20
        ),
        cost_estimate=pl.CostEstimate(
            flops=5_400_000_000, bytes_accessed=4_000_000, transcendentals=10_500_000
        ),
    )(
        queries[0], prompt_keys[0], prompt_values[0], resp_keys[0], resp_values[0],
        slot_row, lengths, probe.reshape(QH, HD),
    )
    return attended[None], loss[0, 0]


def solution(mesh):
    return jax.shard_map(
        local,
        mesh=mesh,
        in_specs=(
            P("pair", "blk", None),
            P("pair", "blk", None),
            P("pair", "blk", None),
            P("pair", "blk", None),
            P("pair", "blk", None),
            P("pair", "blk"),
            P("pair", None),
            P(),
        ),
        out_specs=(P("pair", "blk", None), P()),
        check_vma=False,
    )
```
